32 devices in a mesh: space: 8 (over y, x, core), chan: 4 (over z).
Axes of the slice: x: 2, y: 2, z: 4, core: 2. Of those that a mesh axis runs over, the one named last changes fastest.
Arguments:
- positions: float32 [3, 4096], P(None, 'space'), may hold values from -6 to 6
- features: float32 [512, 4096], P('chan', 'space'), may hold values from -6 to 6
- block_counts: int32 [32], P('space'), may hold values from 64 to 128
- pair_table: int32 [3, 512], P(None, 'space'), may hold values from 0 to 31, as said below
- in_weight: float32 [2, 512, 512], P(None, 'chan'), may hold values from -0.25 to 0.25
- filter_weight: float32 [2, 8, 512], P(None, None, 'chan'), may hold values from -0.125 to 0.125
- mix_weight: float32 [2, 512, 512], P(None, None, 'chan'), may hold values from -0.25 to 0.25
Outputs:
- updated: float32 [512, 4096], P('chan', 'space')
The draws below stay inside these ranges and needn't reach their ends.
Inputs may be any that keep to these rules, and one draw needn't show every extreme that they name: `pair_table`: blocks n * 4 to (n + 1) * 4 - 1 lie on device n along space. In slot p of device d's pair slots the first block is one of device d's blocks and the second a block of device (d + o) mod the number of devices along space, with o from 0 to 2; the third row is 0 or 1. On every device the first 3 slots are live and slot o (o = 0 .. 2) names a second block on device d + o; any live slots follow them, empty slots come last.
All inputs are finite; a program needn't handle non-finite values.
Results may differ from the reference program's by a relative error of at most 0.0003.
Values sent between devices are 32-bit elements; how exact they have to be, the bound alone decides.
A program may use at most 64 MiB of HBM per device.

```python
import jax
import jax.numpy as jnp
from jax import lax

F = 512
K = 8
BLK = 128
LAYERS = 2
PPB = 16
B_DEV = 4
PAIR_DEV = 64
NBLK = 32
ATOMS = 4096
NPAIRS = 512


def draw_pair_table(key, part):
    spatial = NPAIRS // PAIR_DEV
    reach_dev = spatial // 4
    key_shift, key_first, key_second, key_alive = jax.random.split(jax.random.fold_in(key, 17), 4)
    position_id = jnp.arange(NPAIRS, dtype=jnp.int32)
    device = position_id // PAIR_DEV
    slot_at = position_id % PAIR_DEV
    shifts = jax.random.randint(key_shift, (NPAIRS,), 0, reach_dev + 1)
    shifts = jnp.where(slot_at <= reach_dev, slot_at, shifts)
    first_block = device * B_DEV + jax.random.randint(key_first, (NPAIRS,), 0, B_DEV)
    second_block = (device + shifts) % spatial * B_DEV + jax.random.randint(key_second, (NPAIRS,), 0, B_DEV)
    live_count = jax.random.randint(key_alive, (spatial,), PAIR_DEV // 3, PAIR_DEV + 1)
    live_count = jnp.maximum(live_count, reach_dev + 1)
    alive_flag = (slot_at < live_count[device]).astype(jnp.int32)
    return jnp.stack([first_block, second_block, alive_flag]).astype(jnp.int32)


def with_ends(values, key, least, high):
    shape = values.shape
    index_at = [jax.random.randint(jax.random.fold_in(key, axis), (), 0, shape[axis]) for axis in range(len(shape))]
    values = values.at[tuple(index_at)].set(least)
    longest = shape.index(max(shape))
    index_at[longest] = (index_at[longest] + 1) % shape[longest]
    return values.at[tuple(index_at)].set(high)


def block_levels(own_key, shape, cuts, low, top_value):
    gain, own = 1.0, jax.random.fold_in(own_key, 6)
    for axis_at, parts in cuts:
        draws = jnp.exp(jax.random.uniform(jax.random.fold_in(own, axis_at), (parts,), jnp.float32, low / len(cuts), top_value / len(cuts)))
        gain = gain * jnp.repeat(draws, shape[axis_at] // parts).reshape([-1 if axis == axis_at else 1 for axis in range(len(shape))])
    return gain


def gaussian(rng, shape, scale, reach, cuts=(), held_as=jnp.bfloat16):
    drawn = jax.random.normal(rng, shape, jnp.float32) * scale
    if len(cuts) > 0:
        drawn = block_levels(rng, shape, cuts, -0.22, 0.18) * drawn
    return jnp.clip(drawn, min=-reach, max=reach).astype(held_as)


def setup_inputs(seed: int = 0) -> dict:
    keys = jax.random.split(jax.random.key(seed), 8)
    positions = gaussian(keys[0], (3, ATOMS), 1.5, 6.0, ((1, 8),), jnp.float32)
    features = gaussian(keys[1], (F, ATOMS), 1.0, 6.0, ((0, 4), (1, 8)), jnp.float32)
    block_counts = with_ends(jax.random.randint(keys[2], (NBLK,), BLK // 2, BLK + 1), jax.random.fold_in(keys[2], 1), BLK // 2, BLK).astype(jnp.int32)
    pair_table = draw_pair_table(jax.random.fold_in(keys[7], 71), 0)
    in_weight = gaussian(keys[4], (LAYERS, F, F), F ** -0.5, 0.25, ((1, 4),), jnp.float32)
    filter_weight = gaussian(keys[5], (LAYERS, K, F), (PPB * BLK) ** -0.5, 0.125, ((2, 4),), jnp.float32)
    mix_weight = gaussian(keys[6], (LAYERS, F, F), F ** -0.5, 0.25, ((2, 4),), jnp.float32)
    return {"positions": positions, "features": features, "block_counts": block_counts, "pair_table": pair_table, "in_weight": in_weight, "filter_weight": filter_weight, "mix_weight": mix_weight}


cutoff_radius = 6.0
gamma_width = 1.5

def radial_basis(first_geo, second_geo, keep_pair, same_block):
    offsets = first_geo[..., :3, :, None] - second_geo[..., :3, None, :]
    squared = lax.optimization_barrier(jnp.sum(offsets * offsets, axis=-3))
    distance = jnp.sqrt(squared)
    envelope = jnp.where(distance < cutoff_radius, 0.5 * (jnp.cos(jnp.pi * distance / cutoff_radius) + 1.0), 0.0)
    extent = distance.shape[-1]
    diagonal = (lax.broadcasted_iota(jnp.int32, (extent, extent), 0) == lax.broadcasted_iota(jnp.int32, (extent, extent), 1)).astype(jnp.float32)
    allowed = first_geo[..., 3, :, None] * second_geo[..., 3, None, :] * keep_pair[..., None, None] * (1.0 - same_block[..., None, None] * diagonal)
    centers = jnp.arange(K, dtype=jnp.float32) * (cutoff_radius / (K - 1))
    spread = distance[..., None, :, :] - centers[:, None, None]
    return jnp.exp(-gamma_width * spread * spread) * (envelope * allowed)[..., None, :, :]

def reference(positions, features, block_counts, pair_table, in_weight, filter_weight, mix_weight):
    valid = (jnp.arange(BLK, dtype=jnp.int32)[None, :] < block_counts[:, None]).astype(jnp.float32).reshape(1, -1)
    geometry = jnp.concatenate([positions, valid], axis=0)
    state = features
    for layer in range(LAYERS):
        mapped = jnp.dot(in_weight[layer], state, precision=lax.Precision.HIGHEST, preferred_element_type=jnp.float32)
        weights_f = filter_weight[layer]

        def pair_step(collected, column, mapped=mapped, weights_f=weights_f):
            first_start = (column[0] * BLK).astype(jnp.int32)
            second_start = (column[1] * BLK).astype(jnp.int32)
            keep_now = column[2].astype(jnp.float32)
            same_now = (column[0] == column[1]).astype(jnp.float32)
            first_geo = lax.dynamic_slice_in_dim(geometry, first_start, BLK, 1)
            second_geo = lax.dynamic_slice_in_dim(geometry, second_start, BLK, 1)
            basis = radial_basis(first_geo, second_geo, keep_now, same_now)
            first_feat = weights_f[:, :, None] * lax.dynamic_slice_in_dim(mapped, first_start, BLK, 1)[None]
            second_feat = weights_f[:, :, None] * lax.dynamic_slice_in_dim(mapped, second_start, BLK, 1)[None]
            to_first = jnp.einsum('kcj,kij->ci', second_feat, basis, precision=lax.Precision.HIGHEST)
            to_second = jnp.einsum('kci,kij->cj', first_feat, basis, precision=lax.Precision.HIGHEST) * (1.0 - same_now)
            before = lax.dynamic_slice_in_dim(collected, first_start, BLK, 1)
            collected = lax.dynamic_update_slice_in_dim(collected, before + to_first, first_start, 1)
            before = lax.dynamic_slice_in_dim(collected, second_start, BLK, 1)
            collected = lax.dynamic_update_slice_in_dim(collected, before + to_second, second_start, 1)
            return (collected, None)
        messages, unused = lax.scan(pair_step, jnp.zeros(mapped.shape, jnp.float32), pair_table.T)
        mixed = jnp.dot(mix_weight[layer], messages, precision=lax.Precision.HIGHEST, preferred_element_type=jnp.float32)
        state = state + jax.nn.silu(mixed)
    return state
```

```python
import functools
import math

import jax
import jax.numpy as jnp
from jax import lax
from jax.experimental import pallas as pl
from jax.experimental.pallas import tpu as pltpu
from jax.sharding import PartitionSpec as P

K = 8
LAYERS = 2


cutoff_radius = 6.0
gamma_width = 1.5
spacing = cutoff_radius / (K - 1)


def shifted(block, axis, distance):
    devices = range(lax.axis_size(axis))
    route = [((i - distance) % len(devices), i) for i in devices]
    return lax.ppermute(block, axis, route)


def half_cosine(y):
    terms = [(-1) ** n * (math.pi / 2) ** (2 * n) / math.factorial(2 * n) for n in range(8)]
    total = jnp.full_like(y, terms[-1])
    for term in terms[-2::-1]:
        total = total * y + term
    return total


def split_halves(value):
    high = value.astype(jnp.bfloat16)
    low = (value - high.astype(jnp.float32)).astype(jnp.bfloat16)
    return high, low


def write_basis(columns, rows, weight, same, out):
    squared = 0.0
    for axis in range(3):
        offset = columns[:, axis : axis + 1] - rows[axis : axis + 1, :]
        squared = squared + offset * offset
    extent = squared.shape[0]
    limit = cutoff_radius * cutoff_radius
    near = jnp.minimum(squared, limit)
    distance = jnp.sqrt(near)
    root = half_cosine(near * (1.0 / limit))
    allowed = (columns[:, 3:4] * weight) * rows[3:4, :]
    diagonal = lax.broadcasted_iota(jnp.int32, (extent, extent), 0) == lax.broadcasted_iota(
        jnp.int32, (extent, extent), 1
    )
    dropped = (squared >= limit) | (diagonal & same)
    envelope = jnp.where(dropped, 0.0, root * root * allowed)
    middle = K // 2 - 1
    spread = distance - middle * spacing
    centre = jnp.exp(-gamma_width * spread * spread) * envelope
    slope = 2.0 * gamma_width * spacing
    up = jnp.exp(slope * distance)
    down = jnp.exp(-slope * distance)

    def put(k, value):
        high, low = split_halves(value)
        out[k * extent : (k + 1) * extent, :extent] = high
        out[k * extent : (k + 1) * extent, extent:] = low

    put(middle, centre)
    unit = gamma_width * spacing * spacing
    value = centre
    for k in range(middle + 1, K):
        value = value * (up * math.exp(-unit * (2 * k - 1)))
        put(k, value)
    value = centre
    for k in range(middle - 1, -1, -1):
        value = value * (down * math.exp(unit * (2 * k + 1)))
        put(k, value)


def pair_kernel(
    blocks,
    base_ref,
    table_ref,
    columns_ref,
    rows_ref,
    mapped_ref,
    filter_ref,
    out_ref,
    count_s,
    to_s,
    from_s,
    weight_s,
    operand_v,
    basis_a,
    basis_b,
):
    slots, extent, channels = mapped_ref.shape
    spatial = base_ref[1]
    own = base_ref[0]

    def clear(i, carry):
        count_s[i] = 0
        return carry

    lax.fori_loop(0, blocks * slots, clear, 0)

    def tally(p, carry):
        first = table_ref[0, p] - own * blocks
        second = table_ref[1, p]
        holder = second // blocks
        ahead = holder - own
        ahead = jnp.where(ahead < 0, ahead + spatial, ahead)
        second = ahead * blocks + (second - holder * blocks)
        swap = second < first
        at = jnp.where(swap, second, first) * slots + jnp.where(swap, first, second)
        count_s[at] = count_s[at] + table_ref[2, p]
        return carry

    lax.fori_loop(0, table_ref.shape[1], tally, 0)

    def list_row(first, n):
        def list_one(second, n):
            many = count_s[first * slots + second]
            live = (many > 0).astype(jnp.int32)
            other = live * (first != second).astype(jnp.int32)
            weight = many.astype(jnp.float32)
            to_s[n] = first
            from_s[n] = second
            weight_s[n] = weight
            n = n + live
            to_s[n] = second
            from_s[n] = first
            weight_s[n] = weight
            return n + other

        return lax.fori_loop(first, slots, list_one, n)

    total = lax.fori_loop(0, blocks, list_row, 0)
    for extra in range(3):
        to_s[total + extra] = 0
        from_s[total + extra] = 0
        weight_s[total + extra] = 0.0

    for slot in range(slots):
        high, low = split_halves(mapped_ref[slot])
        for part in range(2):
            operand_v[slot, part * extent : (part + 1) * extent, :channels] = high
            operand_v[slot, part * extent : (part + 1) * extent, channels:] = low
    out_ref[...] = jnp.zeros_like(out_ref)

    def build(task, basis):
        to, source = to_s[task], from_s[task]
        write_basis(columns_ref[to], rows_ref[source], weight_s[task], to == source, basis)

    def spend(task, basis):
        to, source = to_s[task], from_s[task]
        product = jnp.dot(basis[...], operand_v[source], preferred_element_type=jnp.float32)
        summed = 0.0
        for k in range(K):
            part = product[k * extent : (k + 1) * extent]
            summed = summed + filter_ref[k : k + 1, :] * (part[:, :channels] + part[:, channels:])
        out_ref[to] = out_ref[to] + summed

    build(0, basis_a)

    def step(turn, carry):
        task = 2 * turn
        build(task + 1, basis_b)
        spend(task, basis_a)
        build(task + 2, basis_a)
        spend(task + 1, basis_b)
        return carry

    lax.fori_loop(0, (total + 1) // 2, step, 0)


def pair_messages(base, table, columns, rows, mapped, filters, blocks, interpret=False):
    slots, extent, channels = mapped.shape
    tasks = 2 * blocks * slots + 8
    smem = pl.BlockSpec(memory_space=pltpu.SMEM)
    vmem = pl.BlockSpec(memory_space=pltpu.VMEM)
    return pl.pallas_call(
        functools.partial(pair_kernel, blocks),
        out_shape=jax.ShapeDtypeStruct(mapped.shape, jnp.float32),
        in_specs=[smem, smem, vmem, vmem, vmem, vmem],
        out_specs=vmem,
        scratch_shapes=[
            pltpu.SMEM((blocks * slots,), jnp.int32),
            pltpu.SMEM((tasks,), jnp.int32),
            pltpu.SMEM((tasks,), jnp.int32),
            pltpu.SMEM((tasks,), jnp.float32),
            pltpu.VMEM((slots, 2 * extent, 2 * channels), jnp.bfloat16),
            pltpu.VMEM((K * extent, 2 * extent), jnp.bfloat16),
            pltpu.VMEM((K * extent, 2 * extent), jnp.bfloat16),
        ],
        compiler_params=pltpu.CompilerParams(vmem_limit_bytes=48 * 1024 * 1024),
        interpret=interpret,
    )(base, table, columns, rows, mapped, filters)


def shards(positions, features, block_counts, pair_table, in_weight, filter_weight, mix_weight):
    spatial = lax.axis_size("space")
    reach_dev = spatial // 4
    own_index = lax.axis_index("space")
    blocks = block_counts.shape[0]
    atoms_dev = positions.shape[1]
    block_len = atoms_dev // blocks
    local_chan = features.shape[0]
    slot_total = (reach_dev + 1) * blocks
    valid = (
        (lax.broadcasted_iota(jnp.int32, (blocks, block_len), 1) < block_counts[:, None])
        .astype(jnp.float32)
        .reshape(1, atoms_dev)
    )
    geometry = jnp.concatenate([positions, valid, jnp.zeros((4, atoms_dev), jnp.float32)], axis=0)
    fetched = [geometry]
    for offset in range(1, reach_dev + 1):
        fetched.append(shifted(geometry, "space", -offset))
    rows = jnp.concatenate(
        [part.reshape(8, blocks, block_len).transpose(1, 0, 2) for part in fetched], axis=0
    )
    columns = rows.transpose(0, 2, 1)
    base = jnp.stack([own_index, jnp.int32(spatial)]).astype(jnp.int32)
    state = features
    for layer in range(LAYERS):
        full_state = lax.all_gather(state, "chan", axis=0, tiled=True)
        mapped = lax.dot_general(
            full_state,
            in_weight[layer],
            (((0,), (1,)), ((), ())),
            precision=lax.Precision.HIGHEST,
            preferred_element_type=jnp.float32,
        )
        neighbours = [mapped]
        for offset in range(1, reach_dev + 1):
            neighbours.append(shifted(mapped, "space", -offset))
        mapped_blocks = jnp.concatenate(neighbours, axis=0).reshape(slot_total, block_len, local_chan)
        collected = pair_messages(
            base, pair_table, columns, rows, mapped_blocks, filter_weight[layer], blocks
        ).reshape(reach_dev + 1, atoms_dev, local_chan)
        received = collected[0]
        for offset in range(1, reach_dev + 1):
            received = received + shifted(collected[offset], "space", offset)
        mixed = lax.dot_general(
            mix_weight[layer],
            received,
            (((1,), (1,)), ((), ())),
            precision=lax.Precision.HIGHEST,
            preferred_element_type=jnp.float32,
        )
        own_mixed = lax.psum_scatter(mixed, "chan", scatter_dimension=0, tiled=True)
        state = state + jax.nn.silu(own_mixed)
    return state


def solution(mesh):
    placed = (
        P(None, "space"),
        P("chan", "space"),
        P("space"),
        P(None, "space"),
        P(None, "chan", None),
        P(None, None, "chan"),
        P(None, None, "chan"),
    )
    return jax.shard_map(
        shards, mesh=mesh, in_specs=placed, out_specs=P("chan", "space"), check_vma=False
    )
```

```python
import functools
import math

import jax
import jax.numpy as jnp
from jax import lax
from jax.experimental import pallas as pl
from jax.experimental.pallas import tpu as pltpu
from jax.sharding import PartitionSpec as P

K = 8
LAYERS = 2


cutoff_radius = 6.0
gamma_width = 1.5
spacing = cutoff_radius / (K - 1)


def shifted(block, axis, distance):
    devices = range(lax.axis_size(axis))
    route = [((i - distance) % len(devices), i) for i in devices]
    return lax.ppermute(block, axis, route)


def half_cosine(y):
    terms = [(-1) ** n * (math.pi / 2) ** (2 * n) / math.factorial(2 * n) for n in range(8)]
    total = jnp.full_like(y, terms[-1])
    for term in terms[-2::-1]:
        total = total * y + term
    return total


def split_halves(value):
    high = value.astype(jnp.bfloat16)
    low = (value - high.astype(jnp.float32)).astype(jnp.bfloat16)
    return high, low


def write_basis(columns, rows, weight, same, out):
    squared = 0.0
    for axis in range(3):
        offset = columns[:, axis : axis + 1] - rows[axis : axis + 1, :]
        squared = squared + offset * offset
    extent = squared.shape[0]
    limit = cutoff_radius * cutoff_radius
    near = jnp.minimum(squared, limit)
    distance = jnp.sqrt(near)
    root = half_cosine(near * (1.0 / limit))
    allowed = (columns[:, 3:4] * weight) * rows[3:4, :]
    diagonal = lax.broadcasted_iota(jnp.int32, (extent, extent), 0) == lax.broadcasted_iota(
        jnp.int32, (extent, extent), 1
    )
    dropped = (squared >= limit) | (diagonal & same)
    envelope = jnp.where(dropped, 0.0, root * root * allowed)
    middle = K // 2 - 1
    spread = distance - middle * spacing
    centre = jnp.exp(-gamma_width * spread * spread) * envelope
    slope = 2.0 * gamma_width * spacing
    up = jnp.exp(slope * distance)
    down = jnp.exp(-slope * distance)

    def put(k, value):
        high, low = split_halves(value)
        out[k * extent : (k + 1) * extent, :extent] = high
        out[k * extent : (k + 1) * extent, extent:] = low

    put(middle, centre)
    unit = gamma_width * spacing * spacing
    value = centre
    for k in range(middle + 1, K):
        value = value * (up * math.exp(-unit * (2 * k - 1)))
        put(k, value)
    value = centre
    for k in range(middle - 1, -1, -1):
        value = value * (down * math.exp(unit * (2 * k + 1)))
        put(k, value)


def pair_kernel(
    blocks,
    base_ref,
    table_ref,
    columns_ref,
    rows_ref,
    mapped_ref,
    filter_ref,
    out_ref,
    count_s,
    to_s,
    from_s,
    weight_s,
    operand_v,
    basis_a,
    basis_b,
):
    slots, extent, channels = mapped_ref.shape
    spatial = base_ref[1]
    own = base_ref[0]

    def clear(i, carry):
        count_s[i] = 0
        return carry

    lax.fori_loop(0, blocks * slots, clear, 0)

    def tally(p, carry):
        first = table_ref[0, p] - own * blocks
        second = table_ref[1, p]
        holder = second // blocks
        ahead = holder - own
        ahead = jnp.where(ahead < 0, ahead + spatial, ahead)
        second = ahead * blocks + (second - holder * blocks)
        swap = second < first
        at = jnp.where(swap, second, first) * slots + jnp.where(swap, first, second)
        count_s[at] = count_s[at] + table_ref[2, p]
        return carry

    lax.fori_loop(0, table_ref.shape[1], tally, 0)

    def list_row(first, n):
        def list_one(second, n):
            many = count_s[first * slots + second]
            live = (many > 0).astype(jnp.int32)
            other = live * (first != second).astype(jnp.int32)
            weight = many.astype(jnp.float32)
            to_s[n] = first
            from_s[n] = second
            weight_s[n] = weight
            n = n + live
            to_s[n] = second
            from_s[n] = first
            weight_s[n] = weight
            return n + other

        return lax.fori_loop(first, slots, list_one, n)

    total = lax.fori_loop(0, blocks, list_row, 0)
    for extra in range(3):
        to_s[total + extra] = 0
        from_s[total + extra] = 0
        weight_s[total + extra] = 0.0

    for slot in range(slots):
        high, low = split_halves(mapped_ref[slot])
        for part in range(2):
            operand_v[slot, part * extent : (part + 1) * extent, :channels] = high
            operand_v[slot, part * extent : (part + 1) * extent, channels:] = low
    out_ref[...] = jnp.zeros_like(out_ref)

    def build(task, basis):
        to, source = to_s[task], from_s[task]
        write_basis(columns_ref[to], rows_ref[source], weight_s[task], to == source, basis)

    def spend(task, basis):
        to, source = to_s[task], from_s[task]
        product = jnp.dot(basis[...], operand_v[source], preferred_element_type=jnp.float32)
        summed = 0.0
        for k in range(K):
            part = product[k * extent : (k + 1) * extent]
            summed = summed + filter_ref[k : k + 1, :] * (part[:, :channels] + part[:, channels:])
        out_ref[to] = out_ref[to] + summed

    build(0, basis_a)

    def step(turn, carry):
        task = 2 * turn
        build(task + 1, basis_b)
        spend(task, basis_a)
        build(task + 2, basis_a)
        spend(task + 1, basis_b)
        return carry

    lax.fori_loop(0, (total + 1) // 2, step, 0)


def pair_messages(base, table, columns, rows, mapped, filters, blocks, interpret=False):
    slots, extent, channels = mapped.shape
    tasks = 2 * blocks * slots + 8
    smem = pl.BlockSpec(memory_space=pltpu.SMEM)
    vmem = pl.BlockSpec(memory_space=pltpu.VMEM)
    return pl.pallas_call(
        functools.partial(pair_kernel, blocks),
        out_shape=jax.ShapeDtypeStruct(mapped.shape, jnp.float32),
        in_specs=[smem, smem, vmem, vmem, vmem, vmem],
        out_specs=vmem,
        scratch_shapes=[
            pltpu.SMEM((blocks * slots,), jnp.int32),
            pltpu.SMEM((tasks,), jnp.int32),
            pltpu.SMEM((tasks,), jnp.int32),
            pltpu.SMEM((tasks,), jnp.float32),
            pltpu.VMEM((slots, 2 * extent, 2 * channels), jnp.bfloat16),
            pltpu.VMEM((K * extent, 2 * extent), jnp.bfloat16),
            pltpu.VMEM((K * extent, 2 * extent), jnp.bfloat16),
        ],
        compiler_params=pltpu.CompilerParams(vmem_limit_bytes=48 * 1024 * 1024),
        interpret=interpret,
    )(base, table, columns, rows, mapped, filters)


HIGHEST = lax.Precision.HIGHEST
MESH = pl.DeviceIdType.MESH


def contract(left, right, left_dim, right_dim):
    return lax.dot_general(
        left,
        right,
        (((left_dim,), (right_dim,)), ((), ())),
        precision=HIGHEST,
        preferred_element_type=jnp.float32,
    )


def greet(reach):
    space, chan = lax.axis_index("space"), lax.axis_index("chan")
    spatial, groups = lax.axis_size("space"), lax.axis_size("chan")
    barrier = pltpu.get_barrier_semaphore()
    partners = [(space, lax.rem(chan + p, groups)) for p in range(1, groups)]
    for offset in range(1, reach + 1):
        partners.append((lax.rem(space + offset, spatial), chan))
        partners.append((lax.rem(space + spatial - offset, spatial), chan))
    for partner in partners:
        pl.semaphore_signal(barrier, inc=1, device_id=partner, device_id_type=MESH)
    pl.semaphore_wait(barrier, len(partners))
    return space, chan, spatial, groups


def send(source, target, sems, at, device):
    copy = pltpu.make_async_remote_copy(
        src_ref=source,
        dst_ref=target,
        send_sem=sems[0].at[at],
        recv_sem=sems[1].at[at],
        device_id=device,
        device_id_type=MESH,
    )
    copy.start()
    return copy


def spread_block(out_ref, block, p, reach, blocks, place, sems):
    space, chan, spatial, groups = place
    copies = []
    for offset in range(1, reach + 1):
        copies.append(
            send(
                out_ref.at[block],
                out_ref.at[offset * blocks + block],
                sems,
                (offset - 1, p),
                (lax.rem(space + spatial - offset, spatial), chan),
            )
        )
    return copies


def gather_kernel(reach, feature_ref, weight_ref, out_ref, state_ref, landed, *sems):
    place = greet(reach)
    space, chan, spatial, groups = place
    chan_sems, space_sems = sems[:2], sems[2:]
    rows, _ = feature_ref.shape
    extent = out_ref.shape[1]
    arriving = {}
    for q in range(groups):
        for p in range(1, groups):
            arriving[p, q] = send(
                feature_ref.at[:, q * extent : (q + 1) * extent],
                landed.at[p - 1, q],
                chan_sems,
                (p - 1, q),
                (space, lax.rem(chan + p, groups)),
            )
    leaving = []
    for q in range(groups):
        total = 0.0
        for p in range(groups):
            if p > 0:
                arriving[p, q].wait_recv()
                part = landed[p - 1, q]
            else:
                part = feature_ref[:, q * extent : (q + 1) * extent]
            source = lax.rem(chan + groups - p, groups)
            columns = pl.ds(pl.multiple_of(source * rows, rows), rows)
            total = total + contract(weight_ref[:, columns], part, 1, 0)
        out_ref[q] = total.T
        leaving += spread_block(out_ref, q, q, reach, groups, place, space_sems)
    own = pl.ds(pl.multiple_of(chan * extent, extent), extent)
    state_ref[chan] = feature_ref[:, own]
    for p in range(1, groups):
        state_ref[lax.rem(chan + groups - p, groups)] = landed[p - 1, chan]
    for copy in arriving.values():
        copy.wait_send()
    for copy in leaving:
        copy.wait()


def mix_states(reach, collected_ref, state_ref, mix_ref, back, sums, heard, place, back_sems, sum_sems):
    space, chan, spatial, groups = place
    order = list(range(1, groups)) + [0]
    copies, returning = [], {}
    for p in order:
        block = lax.rem(chan + p, groups)
        for offset in range(1, reach + 1):
            returning[offset, p] = send(
                collected_ref.at[offset * groups + block],
                back.at[offset - 1, p],
                back_sems,
                (offset - 1, p),
                (lax.rem(space + offset, spatial), chan),
            )
    telling = {}
    for p in order:
        block = lax.rem(chan + p, groups)
        total = collected_ref[block]
        for offset in range(1, reach + 1):
            returning[offset, p].wait_recv()
            total = total + back[offset - 1, p]
        sums[p] = total
        if p > 0:
            telling[p] = send(sums.at[p], heard.at[p - 1], sum_sems, (p - 1,), (space, block))
    copies += list(returning.values()) + list(telling.values())

    def weight(source):
        held = mix_ref[:, source]
        return held.reshape(held.shape[0] * held.shape[1], held.shape[2])

    mixed = contract(weight(chan), sums[0], 1, 1)
    for p in range(1, groups):
        telling[p].wait_recv()
        mixed = mixed + contract(weight(lax.rem(chan + groups - p, groups)), heard[p - 1], 1, 1)
    old = state_ref[...]
    mixed = mixed.reshape(old.shape)
    return old + mixed / (1.0 + jnp.exp(-mixed)), copies


def middle_kernel(
    reach, collected_ref, state_ref, mix_ref, in_ref, out_ref, new_ref, back, sums, heard, ready, *sems
):
    place = greet(reach)
    space, chan, spatial, groups = place
    new_state, copies = mix_states(
        reach, collected_ref, state_ref, mix_ref, back, sums, heard, place, sems[0:2], sems[2:4]
    )
    new_ref[...] = new_state
    flat = new_state.reshape(new_state.shape[0] * new_state.shape[1], new_state.shape[2])
    handing = {}
    for p in list(range(1, groups)) + [0]:
        target = lax.rem(chan + p, groups)
        held = in_ref[:, target]
        held = held.reshape(held.shape[0] * held.shape[1], held.shape[2])
        mapped = contract(held, flat, 1, 0).T
        if p > 0:
            ready[p - 1] = mapped
            handing[p] = send(ready.at[p - 1], out_ref.at[chan], sems[4:6], (p - 1,), (space, target))
        else:
            out_ref[chan] = mapped
    leaving = spread_block(out_ref, chan, 0, reach, groups, place, sems[6:8])
    for p in range(1, groups):
        handing[p].wait_recv()
        block = lax.rem(chan + groups - p, groups)
        leaving += spread_block(out_ref, block, p, reach, groups, place, sems[6:8])
    for copy in copies + list(handing.values()):
        copy.wait_send()
    for copy in leaving:
        copy.wait()


def last_kernel(reach, collected_ref, state_ref, mix_ref, out_ref, back, sums, heard, ready, *sems):
    place = greet(reach)
    space, chan, spatial, groups = place
    new_state, copies = mix_states(
        reach, collected_ref, state_ref, mix_ref, back, sums, heard, place, sems[0:2], sems[2:4]
    )
    ready[...] = new_state
    extent = ready.shape[2]
    own = pl.ds(pl.multiple_of(chan * extent, extent), extent)
    handing = {}
    for p in range(1, groups):
        target = lax.rem(chan + p, groups)
        handing[p] = send(ready.at[target], out_ref.at[:, own], sems[4:6], (p - 1,), (space, target))
    out_ref[:, own] = ready[chan]
    for p in range(1, groups):
        handing[p].wait_recv()
    for copy in copies + list(handing.values()):
        copy.wait_send()


def remote_call(kernel, outs, scratch, pairs, collective, *operands):
    vmem = pl.BlockSpec(memory_space=pltpu.VMEM)
    sems = [pltpu.SemaphoreType.DMA(shape) for shape in pairs for _ in range(2)]
    return pl.pallas_call(
        kernel,
        out_shape=[jax.ShapeDtypeStruct(shape, jnp.float32) for shape in outs],
        in_specs=[vmem] * len(operands),
        out_specs=[vmem] * len(outs),
        scratch_shapes=[pltpu.VMEM(shape, jnp.float32) for shape in scratch] + sems,
        compiler_params=pltpu.CompilerParams(
            collective_id=collective, has_side_effects=True, vmem_limit_bytes=40 * 1024 * 1024
        ),
    )(*operands)


def all_pieces(local, own_index, spatial):
    part = local.shape[0] // spatial
    share = lax.dynamic_slice_in_dim(local, own_index * part, part, 0)
    gathered = lax.all_gather(share, ("space", "chan"), axis=0, tiled=False)
    return gathered.reshape(spatial, lax.axis_size("chan"), part, local.shape[1])


def exchanged_layers(features, mix_weight, in_weight, own_index, reach, blocks, block_len, pairs_of):
    spatial, groups = lax.axis_size("space"), lax.axis_size("chan")
    channels = features.shape[0]
    slots = (reach + 1) * blocks
    mix_full = [all_pieces(mix_weight[0], own_index, spatial)]
    in_full = [None]
    for layer in range(1, LAYERS):
        in_full.append(all_pieces(in_weight[layer], own_index, spatial))
        mix_full.append(all_pieces(mix_weight[layer], own_index, spatial))
    blocked = (slots, block_len, channels)
    held = (groups, channels, block_len)
    square = (block_len, channels)
    mapped, state = remote_call(
        functools.partial(gather_kernel, reach),
        [blocked, held],
        [(groups - 1, groups, channels, block_len)],
        [(groups - 1, groups), (reach, groups)],
        0,
        features,
        in_weight[0],
    )
    scratch = [(reach, groups, *square), (groups, *square), (groups - 1, *square)]
    for layer in range(LAYERS - 1):
        collected = pairs_of(mapped, layer)
        mapped, state = remote_call(
            functools.partial(middle_kernel, reach),
            [blocked, held],
            scratch + [(groups - 1, *square)],
            [(reach, groups), (groups - 1,), (groups - 1,), (reach, groups)],
            1,
            collected,
            state,
            mix_full[layer],
            in_full[layer + 1],
        )
    collected = pairs_of(mapped, LAYERS - 1)
    (updated,) = remote_call(
        functools.partial(last_kernel, reach),
        [features.shape],
        scratch + [held],
        [(reach, groups), (groups - 1,), (groups - 1,)],
        2,
        collected,
        state,
        mix_full[LAYERS - 1],
    )
    return updated


def shards(positions, features, block_counts, pair_table, in_weight, filter_weight, mix_weight):
    spatial = lax.axis_size("space")
    reach_dev = spatial // 4
    own_index = lax.axis_index("space")
    blocks = block_counts.shape[0]
    atoms_dev = positions.shape[1]
    block_len = atoms_dev // blocks
    local_chan = features.shape[0]
    slot_total = (reach_dev + 1) * blocks
    valid = (
        (lax.broadcasted_iota(jnp.int32, (blocks, block_len), 1) < block_counts[:, None])
        .astype(jnp.float32)
        .reshape(1, atoms_dev)
    )
    geometry = jnp.concatenate([positions, valid, jnp.zeros((4, atoms_dev), jnp.float32)], axis=0)
    fetched = [geometry]
    for offset in range(1, reach_dev + 1):
        fetched.append(shifted(geometry, "space", -offset))
    rows = jnp.concatenate(
        [part.reshape(8, blocks, block_len).transpose(1, 0, 2) for part in fetched], axis=0
    )
    columns = rows.transpose(0, 2, 1)
    base = jnp.stack([own_index, jnp.int32(spatial)]).astype(jnp.int32)
    groups = lax.axis_size("chan")

    def pairs_of(mapped_blocks, layer):
        return pair_messages(
            base, pair_table, columns, rows, mapped_blocks, filter_weight[layer], blocks
        )

    whole_tiles = (
        local_chan % 128 == 0
        and block_len % 128 == 0
        and blocks == groups
        and spatial > 2 * reach_dev
        and local_chan % (8 * spatial) == 0
    )
    if whole_tiles:
        return exchanged_layers(
            features, mix_weight, in_weight, own_index, reach_dev, blocks, block_len, pairs_of
        )
    state = features
    for layer in range(LAYERS):
        full_state = lax.all_gather(state, "chan", axis=0, tiled=True)
        mapped = lax.dot_general(
            full_state,
            in_weight[layer],
            (((0,), (1,)), ((), ())),
            precision=lax.Precision.HIGHEST,
            preferred_element_type=jnp.float32,
        )
        neighbours = [mapped]
        for offset in range(1, reach_dev + 1):
            neighbours.append(shifted(mapped, "space", -offset))
        mapped_blocks = jnp.concatenate(neighbours, axis=0).reshape(slot_total, block_len, local_chan)
        collected = pairs_of(mapped_blocks, layer).reshape(reach_dev + 1, atoms_dev, local_chan)
        received = collected[0]
        for offset in range(1, reach_dev + 1):
            received = received + shifted(collected[offset], "space", offset)
        mixed = lax.dot_general(
            mix_weight[layer],
            received,
            (((1,), (1,)), ((), ())),
            precision=lax.Precision.HIGHEST,
            preferred_element_type=jnp.float32,
        )
        own_mixed = lax.psum_scatter(mixed, "chan", scatter_dimension=0, tiled=True)
        state = state + jax.nn.silu(own_mixed)
    return state


def solution(mesh):
    placed = (
        P(None, "space"),
        P("chan", "space"),
        P("space"),
        P(None, "space"),
        P(None, "chan", None),
        P(None, None, "chan"),
        P(None, None, "chan"),
    )
    return jax.shard_map(
        shards, mesh=mesh, in_specs=placed, out_specs=P("chan", "space"), check_vma=False
    )
```

```python
import functools
import math

import jax
import jax.numpy as jnp
from jax import lax
from jax.experimental import pallas as pl
from jax.experimental.pallas import tpu as pltpu
from jax.sharding import PartitionSpec as P

K = 8
LAYERS = 2


cutoff_radius = 6.0
gamma_width = 1.5
spacing = cutoff_radius / (K - 1)


def shifted(block, axis, distance):
    devices = range(lax.axis_size(axis))
    route = [((i - distance) % len(devices), i) for i in devices]
    return lax.ppermute(block, axis, route)


def half_cosine(y):
    terms = [(-1) ** n * (math.pi / 2) ** (2 * n) / math.factorial(2 * n) for n in range(8)]
    total = jnp.full_like(y, terms[-1])
    for term in terms[-2::-1]:
        total = total * y + term
    return total


def split_halves(value):
    high = value.astype(jnp.bfloat16)
    low = (value - high.astype(jnp.float32)).astype(jnp.bfloat16)
    return high, low


def write_basis(columns, rows, weight, same, out):
    squared = 0.0
    for axis in range(3):
        offset = columns[:, axis : axis + 1] - rows[axis : axis + 1, :]
        squared = squared + offset * offset
    extent = squared.shape[0]
    limit = cutoff_radius * cutoff_radius
    near = jnp.minimum(squared, limit)
    distance = jnp.sqrt(near)
    root = half_cosine(near * (1.0 / limit))
    allowed = (columns[:, 3:4] * weight) * rows[3:4, :]
    diagonal = lax.broadcasted_iota(jnp.int32, (extent, extent), 0) == lax.broadcasted_iota(
        jnp.int32, (extent, extent), 1
    )
    dropped = (squared >= limit) | (diagonal & same)
    envelope = jnp.where(dropped, 0.0, root * root * allowed)
    middle = K // 2 - 1
    spread = distance - middle * spacing
    centre = jnp.exp(-gamma_width * spread * spread) * envelope
    slope = 2.0 * gamma_width * spacing
    up = jnp.exp(slope * distance)
    down = jnp.exp(-slope * distance)

    def put(k, value):
        high, low = split_halves(value)
        out[k * extent : (k + 1) * extent, :extent] = high
        out[k * extent : (k + 1) * extent, extent:] = low

    put(middle, centre)
    unit = gamma_width * spacing * spacing
    value = centre
    for k in range(middle + 1, K):
        value = value * (up * math.exp(-unit * (2 * k - 1)))
        put(k, value)
    value = centre
    for k in range(middle - 1, -1, -1):
        value = value * (down * math.exp(unit * (2 * k + 1)))
        put(k, value)


def pair_kernel(
    blocks,
    base_ref,
    table_ref,
    columns_ref,
    rows_ref,
    mapped_ref,
    filter_ref,
    out_ref,
    count_s,
    to_s,
    from_s,
    weight_s,
    operand_v,
    basis_a,
    basis_b,
):
    slots, extent, channels = mapped_ref.shape
    spatial = base_ref[1]
    own = base_ref[0]

    def clear(i, carry):
        count_s[i] = 0
        return carry

    lax.fori_loop(0, blocks * slots, clear, 0)

    def tally(p, carry):
        first = table_ref[0, p] - own * blocks
        second = table_ref[1, p]
        holder = second // blocks
        ahead = holder - own
        ahead = jnp.where(ahead < 0, ahead + spatial, ahead)
        second = ahead * blocks + (second - holder * blocks)
        swap = second < first
        at = jnp.where(swap, second, first) * slots + jnp.where(swap, first, second)
        count_s[at] = count_s[at] + table_ref[2, p]
        return carry

    lax.fori_loop(0, table_ref.shape[1], tally, 0)

    def list_row(first, n):
        def list_one(second, n):
            many = count_s[first * slots + second]
            live = (many > 0).astype(jnp.int32)
            other = live * (first != second).astype(jnp.int32)
            weight = many.astype(jnp.float32)
            to_s[n] = first
            from_s[n] = second
            weight_s[n] = weight
            n = n + live
            to_s[n] = second
            from_s[n] = first
            weight_s[n] = weight
            return n + other

        return lax.fori_loop(first, slots, list_one, n)

    total = lax.fori_loop(0, blocks, list_row, 0)
    for extra in range(3):
        to_s[total + extra] = 0
        from_s[total + extra] = 0
        weight_s[total + extra] = 0.0

    for slot in range(slots):
        high, low = split_halves(mapped_ref[slot])
        for part in range(2):
            operand_v[slot, part * extent : (part + 1) * extent, :channels] = high
            operand_v[slot, part * extent : (part + 1) * extent, channels:] = low
    out_ref[...] = jnp.zeros_like(out_ref)

    def build(task, basis):
        to, source = to_s[task], from_s[task]
        write_basis(columns_ref[to], rows_ref[source], weight_s[task], to == source, basis)

    def spend(task, basis):
        to, source = to_s[task], from_s[task]
        product = jnp.dot(basis[...], operand_v[source], preferred_element_type=jnp.float32)
        summed = 0.0
        for k in range(K):
            part = product[k * extent : (k + 1) * extent]
            summed = summed + filter_ref[k : k + 1, :] * (part[:, :channels] + part[:, channels:])
        out_ref[to] = out_ref[to] + summed

    build(0, basis_a)

    def step(turn, carry):
        task = 2 * turn
        build(task + 1, basis_b)
        spend(task, basis_a)
        build(task + 2, basis_a)
        spend(task + 1, basis_b)
        return carry

    lax.fori_loop(0, (total + 1) // 2, step, 0)


def pair_messages(base, table, columns, rows, mapped, filters, blocks, interpret=False):
    slots, extent, channels = mapped.shape
    tasks = 2 * blocks * slots + 8
    smem = pl.BlockSpec(memory_space=pltpu.SMEM)
    vmem = pl.BlockSpec(memory_space=pltpu.VMEM)
    return pl.pallas_call(
        functools.partial(pair_kernel, blocks),
        out_shape=jax.ShapeDtypeStruct(mapped.shape, jnp.float32),
        in_specs=[smem, smem, vmem, vmem, vmem, vmem],
        out_specs=vmem,
        scratch_shapes=[
            pltpu.SMEM((blocks * slots,), jnp.int32),
            pltpu.SMEM((tasks,), jnp.int32),
            pltpu.SMEM((tasks,), jnp.int32),
            pltpu.SMEM((tasks,), jnp.float32),
            pltpu.VMEM((slots, 2 * extent, 2 * channels), jnp.bfloat16),
            pltpu.VMEM((K * extent, 2 * extent), jnp.bfloat16),
            pltpu.VMEM((K * extent, 2 * extent), jnp.bfloat16),
        ],
        compiler_params=pltpu.CompilerParams(vmem_limit_bytes=48 * 1024 * 1024),
        interpret=interpret,
    )(base, table, columns, rows, mapped, filters)


HIGHEST = lax.Precision.HIGHEST
MESH = pl.DeviceIdType.MESH


def contract(left, right, left_dim, right_dim):
    return lax.dot_general(
        left,
        right,
        (((left_dim,), (right_dim,)), ((), ())),
        precision=HIGHEST,
        preferred_element_type=jnp.float32,
    )


def greet(reach, stride=None):
    space, chan = lax.axis_index("space"), lax.axis_index("chan")
    spatial, groups = lax.axis_size("space"), lax.axis_size("chan")
    barrier = pltpu.get_barrier_semaphore()
    partners = [(space, lax.rem(chan + p, groups)) for p in range(1, groups)]
    offsets = set(range(1, reach + 1)) | {spatial - offset for offset in range(1, reach + 1)}
    if stride is not None:
        offsets |= set(range(stride, spatial, stride))
    for offset in sorted(offsets):
        partners.append((lax.rem(space + offset, spatial), chan))
    for partner in partners:
        pl.semaphore_signal(barrier, inc=1, device_id=partner, device_id_type=MESH)
    pl.semaphore_wait(barrier, len(partners))
    return space, chan, spatial, groups


def send(source, target, sems, at, device):
    copy = pltpu.make_async_remote_copy(
        src_ref=source,
        dst_ref=target,
        send_sem=sems[0].at[at],
        recv_sem=sems[1].at[at],
        device_id=device,
        device_id_type=MESH,
    )
    copy.start()
    return copy


def spread_block(out_ref, block, p, reach, blocks, place, sems):
    space, chan, spatial, groups = place
    copies = []
    for offset in range(1, reach + 1):
        copies.append(
            send(
                out_ref.at[block],
                out_ref.at[offset * blocks + block],
                sems,
                (offset - 1, p),
                (lax.rem(space + spatial - offset, spatial), chan),
            )
        )
    return copies


def gather_kernel(
    reach,
    geometry_ref,
    feature_ref,
    weight_ref,
    mix_ref,
    out_ref,
    state_ref,
    rows_ref,
    columns_ref,
    all_mix_ref,
    all_in_ref,
    landed,
    *sems,
):
    place = greet(reach, 2)
    space, chan, spatial, groups = place
    chan_sems, space_sems, near_sems, piece_sems, far_sems, pair_sems = (
        sems[2 * i : 2 * i + 2] for i in range(6)
    )
    rows, _ = feature_ref.shape
    extent = out_ref.shape[1]
    blocks = geometry_ref.shape[0]

    shares = []
    for source, target in ((mix_ref, all_mix_ref), (weight_ref, all_in_ref)):
        part = target.shape[-2]
        mine = pl.ds(pl.multiple_of(space * part, part), part)
        if target is all_in_ref:
            held = source.at[pl.ds(1, LAYERS - 1), mine]
        else:
            held = source.at[:, mine]
        shares.append((held, target))
    pieces, leaving = [], []
    for p in range(1, groups):
        for kind, (held, target) in enumerate(shares):
            pieces.append(
                send(
                    held,
                    target.at[space, chan],
                    piece_sems,
                    (kind, p - 1),
                    (space, lax.rem(chan + p, groups)),
                )
            )
    rows_ref[:blocks] = geometry_ref[...]
    for offset in range(1, reach + 1):
        leaving.append(
            send(
                geometry_ref,
                rows_ref.at[pl.ds(offset * blocks, blocks)],
                near_sems,
                (offset - 1,),
                (lax.rem(space + spatial - offset, spatial), chan),
            )
        )
    arriving = {}

    def tell(q):
        for p in range(1, groups):
            arriving[p, q] = send(
                feature_ref.at[:, q * extent : (q + 1) * extent],
                landed.at[p - 1, q],
                chan_sems,
                (p - 1, q),
                (space, lax.rem(chan + p, groups)),
            )

    tell(0)
    for held, target in shares:
        target[space, chan] = held[...]
    for copy in pieces:
        copy.wait_recv()
    far, paired = [], []
    partner = (space + 1 - 2 * lax.rem(space, 2), chan)
    for kind, (_, target) in enumerate(shares):
        for hop in range(1, spatial // 2):
            far.append(
                (
                    send(
                        target.at[space],
                        target.at[space],
                        far_sems,
                        (kind, hop - 1),
                        (lax.rem(space + 2 * hop, spatial), chan),
                    ),
                    kind,
                    hop,
                )
            )
        paired.append(send(target.at[space], target.at[space], pair_sems, (kind, 0), partner))
    for q in range(1, groups):
        tell(q)
    for q in range(groups):
        total = 0.0
        for p in range(groups):
            if p > 0:
                arriving[p, q].wait_recv()
                part = landed[p - 1, q]
            else:
                part = feature_ref[:, q * extent : (q + 1) * extent]
            source = lax.rem(chan + groups - p, groups)
            columns = pl.ds(pl.multiple_of(source * rows, rows), rows)
            total = total + contract(weight_ref[0, :, columns], part, 1, 0)
        out_ref[q] = total.T
        leaving += spread_block(out_ref, q, q, reach, groups, place, space_sems)
    own = pl.ds(pl.multiple_of(chan * extent, extent), extent)
    state_ref[chan] = feature_ref[:, own]
    for p in range(1, groups):
        state_ref[lax.rem(chan + groups - p, groups)] = landed[p - 1, chan]
    for copy, kind, hop in far:
        copy.wait_recv()
        source = lax.rem(space + spatial - 2 * hop, spatial)
        target = shares[kind][1]
        paired.append(send(target.at[source], target.at[source], pair_sems, (kind, hop), partner))
    for copy in leaving + paired:
        copy.wait()
    for at in range(rows_ref.shape[0]):
        columns_ref[at] = rows_ref[at].T
    for copy in list(arriving.values()) + pieces + [copy for copy, _, _ in far]:
        copy.wait_send()


def mix_states(reach, layer, collected_ref, state_ref, mix_ref, back, sums, heard, place, back_sems, sum_sems):
    space, chan, spatial, groups = place
    order = list(range(1, groups)) + [0]
    copies, returning = [], {}
    for p in order:
        block = lax.rem(chan + p, groups)
        for offset in range(1, reach + 1):
            returning[offset, p] = send(
                collected_ref.at[offset * groups + block],
                back.at[offset - 1, p],
                back_sems,
                (offset - 1, p),
                (lax.rem(space + offset, spatial), chan),
            )
    telling = {}
    for p in order:
        block = lax.rem(chan + p, groups)
        total = collected_ref[block]
        for offset in range(1, reach + 1):
            returning[offset, p].wait_recv()
            total = total + back[offset - 1, p]
        sums[p] = total
        if p > 0:
            telling[p] = send(sums.at[p], heard.at[p - 1], sum_sems, (p - 1,), (space, block))
    copies += list(returning.values()) + list(telling.values())

    def weight(source):
        held = mix_ref[:, source, layer]
        return held.reshape(held.shape[0] * held.shape[1], held.shape[2])

    mixed = contract(weight(chan), sums[0], 1, 1)
    for p in range(1, groups):
        telling[p].wait_recv()
        mixed = mixed + contract(weight(lax.rem(chan + groups - p, groups)), heard[p - 1], 1, 1)
    old = state_ref[...]
    mixed = mixed.reshape(old.shape)
    return old + mixed / (1.0 + jnp.exp(-mixed)), copies


def middle_kernel(
    reach,
    layer,
    collected_ref,
    state_ref,
    mix_ref,
    in_ref,
    out_ref,
    new_ref,
    back,
    sums,
    heard,
    ready,
    *sems,
):
    place = greet(reach)
    space, chan, spatial, groups = place
    new_state, copies = mix_states(
        reach, layer, collected_ref, state_ref, mix_ref, back, sums, heard, place, sems[0:2], sems[2:4]
    )
    new_ref[...] = new_state
    flat = new_state.reshape(new_state.shape[0] * new_state.shape[1], new_state.shape[2])
    handing = {}
    for p in list(range(1, groups)) + [0]:
        target = lax.rem(chan + p, groups)
        held = in_ref[:, target, layer]
        held = held.reshape(held.shape[0] * held.shape[1], held.shape[2])
        mapped = contract(held, flat, 1, 0).T
        if p > 0:
            ready[p - 1] = mapped
            handing[p] = send(ready.at[p - 1], out_ref.at[chan], sems[4:6], (p - 1,), (space, target))
        else:
            out_ref[chan] = mapped
    leaving = spread_block(out_ref, chan, 0, reach, groups, place, sems[6:8])
    for p in range(1, groups):
        handing[p].wait_recv()
        block = lax.rem(chan + groups - p, groups)
        leaving += spread_block(out_ref, block, p, reach, groups, place, sems[6:8])
    for copy in copies + list(handing.values()):
        copy.wait_send()
    for copy in leaving:
        copy.wait()


def last_kernel(reach, layer, collected_ref, state_ref, mix_ref, out_ref, back, sums, heard, ready, *sems):
    place = greet(reach)
    space, chan, spatial, groups = place
    new_state, copies = mix_states(
        reach, layer, collected_ref, state_ref, mix_ref, back, sums, heard, place, sems[0:2], sems[2:4]
    )
    ready[...] = new_state
    extent = ready.shape[2]
    own = pl.ds(pl.multiple_of(chan * extent, extent), extent)
    handing = {}
    for p in range(1, groups):
        target = lax.rem(chan + p, groups)
        handing[p] = send(ready.at[target], out_ref.at[:, own], sems[4:6], (p - 1,), (space, target))
    out_ref[:, own] = ready[chan]
    for p in range(1, groups):
        handing[p].wait_recv()
    for copy in copies + list(handing.values()):
        copy.wait_send()


def remote_call(kernel, outs, scratch, pairs, collective, *operands):
    vmem = pl.BlockSpec(memory_space=pltpu.VMEM)
    sems = [pltpu.SemaphoreType.DMA(shape) for shape in pairs for _ in range(2)]
    return pl.pallas_call(
        kernel,
        out_shape=[jax.ShapeDtypeStruct(shape, jnp.float32) for shape in outs],
        in_specs=[vmem] * len(operands),
        out_specs=[vmem] * len(outs),
        scratch_shapes=[pltpu.VMEM(shape, jnp.float32) for shape in scratch] + sems,
        compiler_params=pltpu.CompilerParams(
            collective_id=collective, has_side_effects=True, vmem_limit_bytes=40 * 1024 * 1024
        ),
    )(*operands)


def exchanged_layers(geometry, features, in_weight, mix_weight, reach, pairs_of):
    spatial, groups = lax.axis_size("space"), lax.axis_size("chan")
    blocks, _, block_len = geometry.shape
    channels = features.shape[0]
    slots = (reach + 1) * blocks
    blocked = (slots, block_len, channels)
    held = (groups, channels, block_len)
    square = (block_len, channels)
    hops = spatial // 2
    mix_part = mix_weight.shape[1] // spatial
    in_part = in_weight.shape[1] // spatial
    mapped, state, rows, columns, all_mix, all_in = remote_call(
        functools.partial(gather_kernel, reach),
        [
            blocked,
            held,
            (slots, 8, block_len),
            (slots, block_len, 8),
            (spatial, groups, LAYERS, mix_part, mix_weight.shape[2]),
            (spatial, groups, LAYERS - 1, in_part, in_weight.shape[2]),
        ],
        [(groups - 1, groups, channels, block_len)],
        [
            (groups - 1, groups),
            (reach, groups),
            (reach,),
            (2, groups - 1),
            (2, hops - 1),
            (2, hops),
        ],
        0,
        geometry,
        features,
        in_weight,
        mix_weight,
    )
    scratch = [(reach, groups, *square), (groups, *square), (groups - 1, *square)]
    for layer in range(LAYERS - 1):
        collected = pairs_of(columns, rows, mapped, layer)
        mapped, state = remote_call(
            functools.partial(middle_kernel, reach, layer),
            [blocked, held],
            scratch + [(groups - 1, *square)],
            [(reach, groups), (groups - 1,), (groups - 1,), (reach, groups)],
            1,
            collected,
            state,
            all_mix,
            all_in,
        )
    collected = pairs_of(columns, rows, mapped, LAYERS - 1)
    (updated,) = remote_call(
        functools.partial(last_kernel, reach, LAYERS - 1),
        [features.shape],
        scratch + [held],
        [(reach, groups), (groups - 1,), (groups - 1,)],
        2,
        collected,
        state,
        all_mix,
    )
    return updated


def shards(positions, features, block_counts, pair_table, in_weight, filter_weight, mix_weight):
    spatial = lax.axis_size("space")
    reach_dev = spatial // 4
    own_index = lax.axis_index("space")
    blocks = block_counts.shape[0]
    atoms_dev = positions.shape[1]
    block_len = atoms_dev // blocks
    local_chan = features.shape[0]
    slot_total = (reach_dev + 1) * blocks
    valid = (
        (lax.broadcasted_iota(jnp.int32, (blocks, block_len), 1) < block_counts[:, None])
        .astype(jnp.float32)
        .reshape(1, atoms_dev)
    )
    geometry = jnp.concatenate([positions, valid, jnp.zeros((4, atoms_dev), jnp.float32)], axis=0)
    geometry = geometry.reshape(8, blocks, block_len).transpose(1, 0, 2)
    base = jnp.stack([own_index, jnp.int32(spatial)]).astype(jnp.int32)
    groups = lax.axis_size("chan")

    def pairs_of(columns, rows, mapped_blocks, layer):
        return pair_messages(
            base, pair_table, columns, rows, mapped_blocks, filter_weight[layer], blocks
        )

    whole_tiles = (
        local_chan % 128 == 0
        and block_len % 128 == 0
        and blocks == groups
        and spatial > 2 * reach_dev
        and spatial % 2 == 0
        and local_chan % (8 * spatial) == 0
    )
    if whole_tiles:
        return exchanged_layers(geometry, features, in_weight, mix_weight, reach_dev, pairs_of)
    fetched = [geometry]
    for offset in range(1, reach_dev + 1):
        fetched.append(shifted(geometry, "space", -offset))
    rows = jnp.concatenate(fetched, axis=0)
    columns = rows.transpose(0, 2, 1)
    state = features
    for layer in range(LAYERS):
        full_state = lax.all_gather(state, "chan", axis=0, tiled=True)
        mapped = lax.dot_general(
            full_state,
            in_weight[layer],
            (((0,), (1,)), ((), ())),
            precision=lax.Precision.HIGHEST,
            preferred_element_type=jnp.float32,
        )
        neighbours = [mapped]
        for offset in range(1, reach_dev + 1):
            neighbours.append(shifted(mapped, "space", -offset))
        mapped_blocks = jnp.concatenate(neighbours, axis=0).reshape(slot_total, block_len, local_chan)
        collected = pairs_of(columns, rows, mapped_blocks, layer).reshape(reach_dev + 1, atoms_dev, local_chan)
        received = collected[0]
        for offset in range(1, reach_dev + 1):
            received = received + shifted(collected[offset], "space", offset)
        mixed = lax.dot_general(
            mix_weight[layer],
            received,
            (((1,), (1,)), ((), ())),
            precision=lax.Precision.HIGHEST,
            preferred_element_type=jnp.float32,
        )
        own_mixed = lax.psum_scatter(mixed, "chan", scatter_dimension=0, tiled=True)
        state = state + jax.nn.silu(own_mixed)
    return state


def solution(mesh):
    placed = (
        P(None, "space"),
        P("chan", "space"),
        P("space"),
        P(None, "space"),
        P(None, "chan", None),
        P(None, None, "chan"),
        P(None, None, "chan"),
    )
    return jax.shard_map(
        shards, mesh=mesh, in_specs=placed, out_specs=P("chan", "space"), check_vma=False
    )
```

```python
import functools
import math

import jax
import jax.numpy as jnp
from jax import lax
from jax.experimental import pallas as pl
from jax.experimental.pallas import tpu as pltpu
from jax.sharding import PartitionSpec as P

K = 8
LAYERS = 2


cutoff_radius = 6.0
gamma_width = 1.5
spacing = cutoff_radius / (K - 1)


def shifted(block, axis, distance):
    devices = range(lax.axis_size(axis))
    route = [((i - distance) % len(devices), i) for i in devices]
    return lax.ppermute(block, axis, route)


def half_cosine(y):
    terms = [(-1) ** n * (math.pi / 2) ** (2 * n) / math.factorial(2 * n) for n in range(8)]
    total = jnp.full_like(y, terms[-1])
    for term in terms[-2::-1]:
        total = total * y + term
    return total


def split_halves(value):
    high = value.astype(jnp.bfloat16)
    low = (value - high.astype(jnp.float32)).astype(jnp.bfloat16)
    return high, low


def write_basis(columns, rows, weight, same, out):
    squared = 0.0
    for axis in range(3):
        offset = columns[:, axis : axis + 1] - rows[axis : axis + 1, :]
        squared = squared + offset * offset
    extent = squared.shape[0]
    limit = cutoff_radius * cutoff_radius
    near = jnp.minimum(squared, limit)
    distance = jnp.sqrt(near)
    root = half_cosine(near * (1.0 / limit))
    allowed = (columns[:, 3:4] * weight) * rows[3:4, :]
    diagonal = lax.broadcasted_iota(jnp.int32, (extent, extent), 0) == lax.broadcasted_iota(
        jnp.int32, (extent, extent), 1
    )
    dropped = (squared >= limit) | (diagonal & same)
    envelope = jnp.where(dropped, 0.0, root * root * allowed)
    middle = K // 2 - 1
    spread = distance - middle * spacing
    centre = jnp.exp(-gamma_width * spread * spread) * envelope
    slope = 2.0 * gamma_width * spacing
    up = jnp.exp(slope * distance)
    down = jnp.exp(-slope * distance)

    def put(k, value):
        high, low = split_halves(value)
        out[k * extent : (k + 1) * extent, :extent] = high
        out[k * extent : (k + 1) * extent, extent:] = low

    put(middle, centre)
    unit = gamma_width * spacing * spacing
    value = centre
    for k in range(middle + 1, K):
        value = value * (up * math.exp(-unit * (2 * k - 1)))
        put(k, value)
    value = centre
    for k in range(middle - 1, -1, -1):
        value = value * (down * math.exp(unit * (2 * k + 1)))
        put(k, value)


def pair_kernel(
    blocks,
    base_ref,
    table_ref,
    columns_ref,
    rows_ref,
    mapped_ref,
    filter_ref,
    turned_ref,
    out_ref,
    count_s,
    to_s,
    from_s,
    weight_s,
    operand_v,
    scaled_v,
    other_v,
    basis_a,
    basis_b,
):
    slots, extent, channels = mapped_ref.shape
    spatial = base_ref[1]
    own = base_ref[0]

    def clear(i, carry):
        count_s[i] = 0
        return carry

    lax.fori_loop(0, blocks * slots, clear, 0)

    def tally(p, carry):
        first = table_ref[0, p] - own * blocks
        second = table_ref[1, p]
        holder = second // blocks
        ahead = holder - own
        ahead = jnp.where(ahead < 0, ahead + spatial, ahead)
        second = ahead * blocks + (second - holder * blocks)
        swap = second < first
        at = jnp.where(swap, second, first) * slots + jnp.where(swap, first, second)
        count_s[at] = count_s[at] + table_ref[2, p]
        return carry

    lax.fori_loop(0, table_ref.shape[1], tally, 0)

    def list_row(first, n):
        def list_one(second, n):
            many = count_s[first * slots + second]
            to_s[n] = first
            from_s[n] = second
            weight_s[n] = many.astype(jnp.float32)
            return n + (many > 0).astype(jnp.int32)

        return lax.fori_loop(first, slots, list_one, n)

    total = lax.fori_loop(0, blocks, list_row, 0)
    for extra in range(3):
        to_s[total + extra] = 0
        from_s[total + extra] = 0
        weight_s[total + extra] = 0.0

    for slot in range(slots):
        high, low = split_halves(mapped_ref[slot])
        for part in range(2):
            operand_v[slot, part * extent : (part + 1) * extent, :channels] = high
            operand_v[slot, part * extent : (part + 1) * extent, channels:] = low
    for slot in range(blocks):
        turned = mapped_ref[slot].T
        for k in range(K):
            high, low = split_halves(turned * turned_ref[:, k : k + 1])
            scaled_v[slot, :channels, k * extent : (k + 1) * extent] = high
            scaled_v[slot, channels:, k * extent : (k + 1) * extent] = low
    out_ref[...] = jnp.zeros_like(out_ref)
    other_v[...] = jnp.zeros_like(other_v)

    def build(task, basis):
        to, source = to_s[task], from_s[task]
        write_basis(columns_ref[to], rows_ref[source], weight_s[task], to == source, basis)

    def spend(task, basis):
        to, source = to_s[task], from_s[task]
        product = jnp.dot(basis[...], operand_v[source], preferred_element_type=jnp.float32)
        summed = 0.0
        for k in range(K):
            part = product[k * extent : (k + 1) * extent]
            summed = summed + filter_ref[k : k + 1, :] * (part[:, :channels] + part[:, channels:])
        out_ref[to] = out_ref[to] + summed
        both = jnp.dot(scaled_v[to], basis[...], preferred_element_type=jnp.float32)
        back = both[:channels] + both[channels:]
        back = back[:, :extent] + back[:, extent:]
        other_v[source] = other_v[source] + back * jnp.where(to == source, 0.0, 1.0)

    build(0, basis_a)

    def step(turn, carry):
        task = 2 * turn
        build(task + 1, basis_b)
        spend(task, basis_a)
        build(task + 2, basis_a)
        spend(task + 1, basis_b)
        return carry

    lax.fori_loop(0, (total + 1) // 2, step, 0)
    for slot in range(slots):
        out_ref[slot] = out_ref[slot] + other_v[slot].T


def pair_messages(base, table, columns, rows, mapped, filters, blocks, interpret=False):
    slots, extent, channels = mapped.shape
    tasks = blocks * slots + 8
    smem = pl.BlockSpec(memory_space=pltpu.SMEM)
    vmem = pl.BlockSpec(memory_space=pltpu.VMEM)
    return pl.pallas_call(
        functools.partial(pair_kernel, blocks),
        out_shape=jax.ShapeDtypeStruct(mapped.shape, jnp.float32),
        in_specs=[smem, smem, vmem, vmem, vmem, vmem, vmem],
        out_specs=vmem,
        scratch_shapes=[
            pltpu.SMEM((blocks * slots,), jnp.int32),
            pltpu.SMEM((tasks,), jnp.int32),
            pltpu.SMEM((tasks,), jnp.int32),
            pltpu.SMEM((tasks,), jnp.float32),
            pltpu.VMEM((slots, 2 * extent, 2 * channels), jnp.bfloat16),
            pltpu.VMEM((blocks, 2 * channels, K * extent), jnp.bfloat16),
            pltpu.VMEM((slots, channels, extent), jnp.float32),
            pltpu.VMEM((K * extent, 2 * extent), jnp.bfloat16),
            pltpu.VMEM((K * extent, 2 * extent), jnp.bfloat16),
        ],
        compiler_params=pltpu.CompilerParams(vmem_limit_bytes=48 * 1024 * 1024),
        interpret=interpret,
    )(base, table, columns, rows, mapped, filters, filters.T)


HIGHEST = lax.Precision.HIGHEST
MESH = pl.DeviceIdType.MESH


def contract(left, right, left_dim, right_dim):
    return lax.dot_general(
        left,
        right,
        (((left_dim,), (right_dim,)), ((), ())),
        precision=HIGHEST,
        preferred_element_type=jnp.float32,
    )


def greet(reach, stride=None):
    space, chan = lax.axis_index("space"), lax.axis_index("chan")
    spatial, groups = lax.axis_size("space"), lax.axis_size("chan")
    barrier = pltpu.get_barrier_semaphore()
    partners = [(space, lax.rem(chan + p, groups)) for p in range(1, groups)]
    offsets = set(range(1, reach + 1)) | {spatial - offset for offset in range(1, reach + 1)}
    if stride is not None:
        offsets |= set(range(stride, spatial, stride))
    for offset in sorted(offsets):
        partners.append((lax.rem(space + offset, spatial), chan))
    for partner in partners:
        pl.semaphore_signal(barrier, inc=1, device_id=partner, device_id_type=MESH)
    pl.semaphore_wait(barrier, len(partners))
    return space, chan, spatial, groups


def send(source, target, sems, at, device):
    copy = pltpu.make_async_remote_copy(
        src_ref=source,
        dst_ref=target,
        send_sem=sems[0].at[at],
        recv_sem=sems[1].at[at],
        device_id=device,
        device_id_type=MESH,
    )
    copy.start()
    return copy


def spread_block(out_ref, block, p, reach, blocks, place, sems):
    space, chan, spatial, groups = place
    copies = []
    for offset in range(1, reach + 1):
        copies.append(
            send(
                out_ref.at[block],
                out_ref.at[offset * blocks + block],
                sems,
                (offset - 1, p),
                (lax.rem(space + spatial - offset, spatial), chan),
            )
        )
    return copies


def gather_kernel(
    reach,
    geometry_ref,
    feature_ref,
    weight_ref,
    mix_ref,
    out_ref,
    state_ref,
    rows_ref,
    columns_ref,
    all_mix_ref,
    all_in_ref,
    landed,
    feature_v,
    weight_v,
    *sems,
):
    place = greet(reach, 2)
    space, chan, spatial, groups = place
    chan_sems, space_sems, near_sems, piece_sems, far_sems, pair_sems, own_sems = (
        sems[2 * i : 2 * i + 2] for i in range(7)
    )
    fetched = [
        pltpu.make_async_copy(feature_ref, feature_v, own_sems[0].at[0]),
        pltpu.make_async_copy(weight_ref.at[0], weight_v, own_sems[0].at[1]),
    ]
    for copy in fetched:
        copy.start()
    rows, _ = feature_ref.shape
    extent = out_ref.shape[1]
    blocks = geometry_ref.shape[0]

    shares = []
    for source, target in ((mix_ref, all_mix_ref), (weight_ref, all_in_ref)):
        part = target.shape[-2]
        mine = pl.ds(pl.multiple_of(space * part, part), part)
        if target is all_in_ref:
            held = source.at[pl.ds(1, LAYERS - 1), mine]
        else:
            held = source.at[:, mine]
        shares.append((held, target))
    pieces, leaving = [], []
    for p in range(1, groups):
        for kind, (held, target) in enumerate(shares):
            pieces.append(
                send(
                    held,
                    target.at[space, chan],
                    piece_sems,
                    (kind, p - 1),
                    (space, lax.rem(chan + p, groups)),
                )
            )
    rows_ref[:blocks] = geometry_ref[...]
    for offset in range(1, reach + 1):
        leaving.append(
            send(
                geometry_ref,
                rows_ref.at[pl.ds(offset * blocks, blocks)],
                near_sems,
                (offset - 1,),
                (lax.rem(space + spatial - offset, spatial), chan),
            )
        )
    arriving = {}

    def tell(q):
        for p in range(1, groups):
            arriving[p, q] = send(
                feature_ref.at[:, q * extent : (q + 1) * extent],
                landed.at[p - 1, q],
                chan_sems,
                (p - 1, q),
                (space, lax.rem(chan + p, groups)),
            )

    tell(0)
    kept = []
    for kind, (held, target) in enumerate(shares):
        kept.append(pltpu.make_async_copy(held, target.at[space, chan], own_sems[1].at[kind]))
        kept[-1].start()
    for copy in kept:
        copy.wait()
    for copy in pieces:
        copy.wait_recv()
    far, paired = [], []
    partner = (space + 1 - 2 * lax.rem(space, 2), chan)
    for kind, (_, target) in enumerate(shares):
        for hop in range(1, spatial // 2):
            far.append(
                (
                    send(
                        target.at[space],
                        target.at[space],
                        far_sems,
                        (kind, hop - 1),
                        (lax.rem(space + 2 * hop, spatial), chan),
                    ),
                    kind,
                    hop,
                )
            )
        paired.append(send(target.at[space], target.at[space], pair_sems, (kind, 0), partner))
    for q in range(1, groups):
        tell(q)
    for copy in fetched:
        copy.wait()
    for q in range(groups):
        total = 0.0
        for p in range(groups):
            if p > 0:
                arriving[p, q].wait_recv()
                part = landed[p - 1, q]
            else:
                part = feature_v[:, q * extent : (q + 1) * extent]
            source = lax.rem(chan + groups - p, groups)
            columns = pl.ds(pl.multiple_of(source * rows, rows), rows)
            total = total + contract(weight_v[:, columns], part, 1, 0)
        out_ref[q] = total.T
        leaving += spread_block(out_ref, q, q, reach, groups, place, space_sems)
    own = pl.ds(pl.multiple_of(chan * extent, extent), extent)
    state_ref[chan] = feature_v[:, own]
    for p in range(1, groups):
        state_ref[lax.rem(chan + groups - p, groups)] = landed[p - 1, chan]
    for copy, kind, hop in far:
        copy.wait_recv()
        source = lax.rem(space + spatial - 2 * hop, spatial)
        target = shares[kind][1]
        paired.append(send(target.at[source], target.at[source], pair_sems, (kind, hop), partner))
    for copy in leaving + paired:
        copy.wait()
    for at in range(rows_ref.shape[0]):
        columns_ref[at] = rows_ref[at].T
    for copy in list(arriving.values()) + pieces + [copy for copy, _, _ in far]:
        copy.wait_send()


def mix_states(reach, layer, collected_ref, state_ref, mix_ref, back, sums, heard, place, back_sems, sum_sems):
    space, chan, spatial, groups = place
    order = list(range(1, groups)) + [0]
    copies, returning = [], {}
    for p in order:
        block = lax.rem(chan + p, groups)
        for offset in range(1, reach + 1):
            returning[offset, p] = send(
                collected_ref.at[offset * groups + block],
                back.at[offset - 1, p],
                back_sems,
                (offset - 1, p),
                (lax.rem(space + offset, spatial), chan),
            )
    telling = {}
    for p in order:
        block = lax.rem(chan + p, groups)
        total = collected_ref[block]
        for offset in range(1, reach + 1):
            returning[offset, p].wait_recv()
            total = total + back[offset - 1, p]
        sums[p] = total
        if p > 0:
            telling[p] = send(sums.at[p], heard.at[p - 1], sum_sems, (p - 1,), (space, block))
    copies += list(returning.values()) + list(telling.values())

    def weight(source):
        held = mix_ref[:, source, layer]
        return held.reshape(held.shape[0] * held.shape[1], held.shape[2])

    mixed = contract(weight(chan), sums[0], 1, 1)
    for p in range(1, groups):
        telling[p].wait_recv()
        mixed = mixed + contract(weight(lax.rem(chan + groups - p, groups)), heard[p - 1], 1, 1)
    old = state_ref[...]
    mixed = mixed.reshape(old.shape)
    return old + mixed / (1.0 + jnp.exp(-mixed)), copies


def middle_kernel(
    reach,
    layer,
    collected_ref,
    state_ref,
    mix_ref,
    in_ref,
    out_ref,
    new_ref,
    back,
    sums,
    heard,
    ready,
    *sems,
):
    place = greet(reach)
    space, chan, spatial, groups = place
    new_state, copies = mix_states(
        reach, layer, collected_ref, state_ref, mix_ref, back, sums, heard, place, sems[0:2], sems[2:4]
    )
    new_ref[...] = new_state
    flat = new_state.reshape(new_state.shape[0] * new_state.shape[1], new_state.shape[2])
    handing = {}
    for p in list(range(1, groups)) + [0]:
        target = lax.rem(chan + p, groups)
        held = in_ref[:, target, layer]
        held = held.reshape(held.shape[0] * held.shape[1], held.shape[2])
        mapped = contract(held, flat, 1, 0).T
        if p > 0:
            ready[p - 1] = mapped
            handing[p] = send(ready.at[p - 1], out_ref.at[chan], sems[4:6], (p - 1,), (space, target))
        else:
            out_ref[chan] = mapped
    leaving = spread_block(out_ref, chan, 0, reach, groups, place, sems[6:8])
    for p in range(1, groups):
        handing[p].wait_recv()
        block = lax.rem(chan + groups - p, groups)
        leaving += spread_block(out_ref, block, p, reach, groups, place, sems[6:8])
    for copy in copies + list(handing.values()):
        copy.wait_send()
    for copy in leaving:
        copy.wait()


def last_kernel(reach, layer, collected_ref, state_ref, mix_ref, out_ref, back, sums, heard, ready, *sems):
    place = greet(reach)
    space, chan, spatial, groups = place
    new_state, copies = mix_states(
        reach, layer, collected_ref, state_ref, mix_ref, back, sums, heard, place, sems[0:2], sems[2:4]
    )
    ready[...] = new_state
    extent = ready.shape[2]
    own = pl.ds(pl.multiple_of(chan * extent, extent), extent)
    handing = {}
    for p in range(1, groups):
        target = lax.rem(chan + p, groups)
        handing[p] = send(ready.at[target], out_ref.at[:, own], sems[4:6], (p - 1,), (space, target))
    out_ref[:, own] = ready[chan]
    for p in range(1, groups):
        handing[p].wait_recv()
    for copy in copies + list(handing.values()):
        copy.wait_send()


def remote_call(kernel, outs, scratch, pairs, collective, *operands, elsewhere=0):
    vmem = pl.BlockSpec(memory_space=pltpu.VMEM)
    sems = [pltpu.SemaphoreType.DMA(shape) for shape in pairs for _ in range(2)]
    return pl.pallas_call(
        kernel,
        out_shape=[jax.ShapeDtypeStruct(shape, jnp.float32) for shape in outs],
        in_specs=[vmem] * (len(operands) - elsewhere)
        + [pl.BlockSpec(memory_space=pl.ANY)] * elsewhere,
        out_specs=[vmem] * len(outs),
        scratch_shapes=[pltpu.VMEM(shape, jnp.float32) for shape in scratch] + sems,
        compiler_params=pltpu.CompilerParams(
            collective_id=collective, has_side_effects=True, vmem_limit_bytes=40 * 1024 * 1024
        ),
    )(*operands)


def exchanged_layers(geometry, features, in_weight, mix_weight, reach, pairs_of):
    spatial, groups = lax.axis_size("space"), lax.axis_size("chan")
    blocks, _, block_len = geometry.shape
    channels = features.shape[0]
    slots = (reach + 1) * blocks
    blocked = (slots, block_len, channels)
    held = (groups, channels, block_len)
    square = (block_len, channels)
    hops = spatial // 2
    mix_part = mix_weight.shape[1] // spatial
    in_part = in_weight.shape[1] // spatial
    mapped, state, rows, columns, all_mix, all_in = remote_call(
        functools.partial(gather_kernel, reach),
        [
            blocked,
            held,
            (slots, 8, block_len),
            (slots, block_len, 8),
            (spatial, groups, LAYERS, mix_part, mix_weight.shape[2]),
            (spatial, groups, LAYERS - 1, in_part, in_weight.shape[2]),
        ],
        [(groups - 1, groups, channels, block_len), features.shape, in_weight.shape[1:]],
        [
            (groups - 1, groups),
            (reach, groups),
            (reach,),
            (2, groups - 1),
            (2, hops - 1),
            (2, hops),
            (2,),
        ],
        0,
        geometry,
        features,
        in_weight,
        mix_weight,
        elsewhere=3,
    )
    scratch = [(reach, groups, *square), (groups, *square), (groups - 1, *square)]
    for layer in range(LAYERS - 1):
        collected = pairs_of(columns, rows, mapped, layer)
        mapped, state = remote_call(
            functools.partial(middle_kernel, reach, layer),
            [blocked, held],
            scratch + [(groups - 1, *square)],
            [(reach, groups), (groups - 1,), (groups - 1,), (reach, groups)],
            1,
            collected,
            state,
            all_mix,
            all_in,
        )
    collected = pairs_of(columns, rows, mapped, LAYERS - 1)
    (updated,) = remote_call(
        functools.partial(last_kernel, reach, LAYERS - 1),
        [features.shape],
        scratch + [held],
        [(reach, groups), (groups - 1,), (groups - 1,)],
        2,
        collected,
        state,
        all_mix,
    )
    return updated


def shards(positions, features, block_counts, pair_table, in_weight, filter_weight, mix_weight):
    spatial = lax.axis_size("space")
    reach_dev = spatial // 4
    own_index = lax.axis_index("space")
    blocks = block_counts.shape[0]
    atoms_dev = positions.shape[1]
    block_len = atoms_dev // blocks
    local_chan = features.shape[0]
    slot_total = (reach_dev + 1) * blocks
    valid = (
        (lax.broadcasted_iota(jnp.int32, (blocks, block_len), 1) < block_counts[:, None])
        .astype(jnp.float32)
        .reshape(1, atoms_dev)
    )
    geometry = jnp.concatenate([positions, valid, jnp.zeros((4, atoms_dev), jnp.float32)], axis=0)
    geometry = geometry.reshape(8, blocks, block_len).transpose(1, 0, 2)
    base = jnp.stack([own_index, jnp.int32(spatial)]).astype(jnp.int32)
    groups = lax.axis_size("chan")

    def pairs_of(columns, rows, mapped_blocks, layer):
        return pair_messages(
            base, pair_table, columns, rows, mapped_blocks, filter_weight[layer], blocks
        )

    whole_tiles = (
        local_chan % 128 == 0
        and block_len % 128 == 0
        and blocks == groups
        and spatial > 2 * reach_dev
        and spatial % 2 == 0
        and local_chan % (8 * spatial) == 0
    )
    if whole_tiles:
        return exchanged_layers(geometry, features, in_weight, mix_weight, reach_dev, pairs_of)
    fetched = [geometry]
    for offset in range(1, reach_dev + 1):
        fetched.append(shifted(geometry, "space", -offset))
    rows = jnp.concatenate(fetched, axis=0)
    columns = rows.transpose(0, 2, 1)
    state = features
    for layer in range(LAYERS):
        full_state = lax.all_gather(state, "chan", axis=0, tiled=True)
        mapped = lax.dot_general(
            full_state,
            in_weight[layer],
            (((0,), (1,)), ((), ())),
            precision=lax.Precision.HIGHEST,
            preferred_element_type=jnp.float32,
        )
        neighbours = [mapped]
        for offset in range(1, reach_dev + 1):
            neighbours.append(shifted(mapped, "space", -offset))
        mapped_blocks = jnp.concatenate(neighbours, axis=0).reshape(slot_total, block_len, local_chan)
        collected = pairs_of(columns, rows, mapped_blocks, layer).reshape(reach_dev + 1, atoms_dev, local_chan)
        received = collected[0]
        for offset in range(1, reach_dev + 1):
            received = received + shifted(collected[offset], "space", offset)
        mixed = lax.dot_general(
            mix_weight[layer],
            received,
            (((1,), (1,)), ((), ())),
            precision=lax.Precision.HIGHEST,
            preferred_element_type=jnp.float32,
        )
        own_mixed = lax.psum_scatter(mixed, "chan", scatter_dimension=0, tiled=True)
        state = state + jax.nn.silu(own_mixed)
    return state


def solution(mesh):
    placed = (
        P(None, "space"),
        P("chan", "space"),
        P("space"),
        P(None, "space"),
        P(None, "chan", None),
        P(None, None, "chan"),
        P(None, None, "chan"),
    )
    return jax.shard_map(
        shards, mesh=mesh, in_specs=placed, out_specs=P("chan", "space"), check_vma=False
    )
```

```python
import functools
import math

import jax
import jax.numpy as jnp
from jax import lax
from jax.experimental import pallas as pl
from jax.experimental.pallas import tpu as pltpu
from jax.sharding import PartitionSpec as P

K = 8
LAYERS = 2


cutoff_radius = 6.0
gamma_width = 1.5
spacing = cutoff_radius / (K - 1)


def shifted(block, axis, distance):
    devices = range(lax.axis_size(axis))
    route = [((i - distance) % len(devices), i) for i in devices]
    return lax.ppermute(block, axis, route)


def half_cosine(y):
    terms = [(-1) ** n * (math.pi / 2) ** (2 * n) / math.factorial(2 * n) for n in range(8)]
    total = jnp.full_like(y, terms[-1])
    for term in terms[-2::-1]:
        total = total * y + term
    return total


def split_halves(value):
    high = value.astype(jnp.bfloat16)
    low = (value - high.astype(jnp.float32)).astype(jnp.bfloat16)
    return high, low


def write_basis(columns, rows, weight, same, out):
    squared = 0.0
    for axis in range(3):
        offset = columns[:, axis : axis + 1] - rows[axis : axis + 1, :]
        squared = squared + offset * offset
    extent = squared.shape[0]
    limit = cutoff_radius * cutoff_radius
    near = jnp.minimum(squared, limit)
    distance = jnp.sqrt(near)
    root = half_cosine(near * (1.0 / limit))
    allowed = (columns[:, 3:4] * weight) * rows[3:4, :]
    diagonal = lax.broadcasted_iota(jnp.int32, (extent, extent), 0) == lax.broadcasted_iota(
        jnp.int32, (extent, extent), 1
    )
    dropped = (squared >= limit) | (diagonal & same)
    envelope = jnp.where(dropped, 0.0, root * root * allowed)
    middle = K // 2 - 1
    spread = distance - middle * spacing
    centre = jnp.exp(-gamma_width * spread * spread) * envelope
    slope = 2.0 * gamma_width * spacing
    up = jnp.exp(slope * distance)
    down = jnp.exp(-slope * distance)

    def put(k, value):
        high, low = split_halves(value)
        out[k * extent : (k + 1) * extent, :extent] = high
        out[k * extent : (k + 1) * extent, extent:] = low

    put(middle, centre)
    unit = gamma_width * spacing * spacing
    value = centre
    for k in range(middle + 1, K):
        value = value * (up * math.exp(-unit * (2 * k - 1)))
        put(k, value)
    value = centre
    for k in range(middle - 1, -1, -1):
        value = value * (down * math.exp(unit * (2 * k + 1)))
        put(k, value)


def pair_kernel(
    blocks,
    base_ref,
    table_ref,
    columns_ref,
    rows_ref,
    mapped_ref,
    filter_ref,
    turned_ref,
    out_ref,
    count_s,
    to_s,
    from_s,
    weight_s,
    operand_v,
    scaled_v,
    other_v,
    basis_a,
    basis_b,
):
    slots, extent, channels = mapped_ref.shape
    spatial = base_ref[1]
    own = base_ref[0]

    def clear(i, carry):
        count_s[i] = 0
        return carry

    lax.fori_loop(0, blocks * slots, clear, 0)

    def tally(p, carry):
        first = table_ref[0, p] - own * blocks
        second = table_ref[1, p]
        holder = second // blocks
        ahead = holder - own
        ahead = jnp.where(ahead < 0, ahead + spatial, ahead)
        second = ahead * blocks + (second - holder * blocks)
        swap = second < first
        at = jnp.where(swap, second, first) * slots + jnp.where(swap, first, second)
        count_s[at] = count_s[at] + table_ref[2, p]
        return carry

    lax.fori_loop(0, table_ref.shape[1], tally, 0)

    def list_row(first, n):
        def list_one(second, n):
            many = count_s[first * slots + second]
            to_s[n] = first
            from_s[n] = second
            weight_s[n] = many.astype(jnp.float32)
            return n + (many > 0).astype(jnp.int32)

        return lax.fori_loop(first, slots, list_one, n)

    total = lax.fori_loop(0, blocks, list_row, 0)
    for extra in range(3):
        to_s[total + extra] = 0
        from_s[total + extra] = 0
        weight_s[total + extra] = 0.0

    for slot in range(slots):
        high, low = split_halves(mapped_ref[slot])
        for part in range(2):
            operand_v[slot, part * extent : (part + 1) * extent, :channels] = high
            operand_v[slot, part * extent : (part + 1) * extent, channels:] = low
    for slot in range(blocks):
        turned = mapped_ref[slot].T
        for k in range(K):
            high, low = split_halves(turned * turned_ref[:, k : k + 1])
            scaled_v[slot, :channels, k * extent : (k + 1) * extent] = high
            scaled_v[slot, channels:, k * extent : (k + 1) * extent] = low
    out_ref[...] = jnp.zeros_like(out_ref)
    other_v[...] = jnp.zeros_like(other_v)

    def build(task, basis):
        to, source = to_s[task], from_s[task]
        write_basis(columns_ref[to], rows_ref[source], weight_s[task], to == source, basis)

    def spend(task, basis):
        to, source = to_s[task], from_s[task]
        product = jnp.dot(basis[...], operand_v[source], preferred_element_type=jnp.float32)
        summed = 0.0
        for k in range(K):
            part = product[k * extent : (k + 1) * extent]
            summed = summed + filter_ref[k : k + 1, :] * (part[:, :channels] + part[:, channels:])
        out_ref[to] = out_ref[to] + summed
        both = jnp.dot(scaled_v[to], basis[...], preferred_element_type=jnp.float32)
        back = both[:channels] + both[channels:]
        back = back[:, :extent] + back[:, extent:]
        other_v[source] = other_v[source] + back * jnp.where(to == source, 0.0, 1.0)

    build(0, basis_a)

    def step(turn, carry):
        task = 2 * turn
        build(task + 1, basis_b)
        spend(task, basis_a)
        build(task + 2, basis_a)
        spend(task + 1, basis_b)
        return carry

    lax.fori_loop(0, (total + 1) // 2, step, 0)
    for slot in range(slots):
        out_ref[slot] = out_ref[slot] + other_v[slot].T


def pair_messages(base, table, columns, rows, mapped, filters, blocks, interpret=False):
    slots, extent, channels = mapped.shape
    tasks = blocks * slots + 8
    smem = pl.BlockSpec(memory_space=pltpu.SMEM)
    vmem = pl.BlockSpec(memory_space=pltpu.VMEM)
    return pl.pallas_call(
        functools.partial(pair_kernel, blocks),
        out_shape=jax.ShapeDtypeStruct(mapped.shape, jnp.float32),
        in_specs=[smem, smem, vmem, vmem, vmem, vmem, vmem],
        out_specs=vmem,
        scratch_shapes=[
            pltpu.SMEM((blocks * slots,), jnp.int32),
            pltpu.SMEM((tasks,), jnp.int32),
            pltpu.SMEM((tasks,), jnp.int32),
            pltpu.SMEM((tasks,), jnp.float32),
            pltpu.VMEM((slots, 2 * extent, 2 * channels), jnp.bfloat16),
            pltpu.VMEM((blocks, 2 * channels, K * extent), jnp.bfloat16),
            pltpu.VMEM((slots, channels, extent), jnp.float32),
            pltpu.VMEM((K * extent, 2 * extent), jnp.bfloat16),
            pltpu.VMEM((K * extent, 2 * extent), jnp.bfloat16),
        ],
        compiler_params=pltpu.CompilerParams(vmem_limit_bytes=60 * 1024 * 1024),
        interpret=interpret,
    )(base, table, columns, rows, mapped, filters, filters.T)


HIGHEST = lax.Precision.HIGHEST
MESH = pl.DeviceIdType.MESH


def contract(left, right, left_dim, right_dim):
    return lax.dot_general(
        left,
        right,
        (((left_dim,), (right_dim,)), ((), ())),
        precision=HIGHEST,
        preferred_element_type=jnp.float32,
    )


def greet(reach, stride=None):
    space, chan = lax.axis_index("space"), lax.axis_index("chan")
    spatial, groups = lax.axis_size("space"), lax.axis_size("chan")
    barrier = pltpu.get_barrier_semaphore()
    partners = [(space, lax.rem(chan + p, groups)) for p in range(1, groups)]
    offsets = set(range(1, reach + 1)) | {spatial - offset for offset in range(1, reach + 1)}
    if stride is not None:
        offsets |= set(range(stride, spatial, stride))
    for offset in sorted(offsets):
        partners.append((lax.rem(space + offset, spatial), chan))
    for partner in partners:
        pl.semaphore_signal(barrier, inc=1, device_id=partner, device_id_type=MESH)
    pl.semaphore_wait(barrier, len(partners))
    return space, chan, spatial, groups


def send(source, target, sems, at, device):
    copy = pltpu.make_async_remote_copy(
        src_ref=source,
        dst_ref=target,
        send_sem=sems[0].at[at],
        recv_sem=sems[1].at[at],
        device_id=device,
        device_id_type=MESH,
    )
    copy.start()
    return copy


def spread_block(out_ref, block, p, reach, blocks, place, sems):
    space, chan, spatial, groups = place
    copies = []
    for offset in range(1, reach + 1):
        copies.append(
            send(
                out_ref.at[block],
                out_ref.at[offset * blocks + block],
                sems,
                (offset - 1, p),
                (lax.rem(space + spatial - offset, spatial), chan),
            )
        )
    return copies


class Line:
    def __init__(self, place, sems):
        self.space, self.chan, _, self.groups = place
        self.sems = sems
        self.sent = []
        near = [p for far in range(1, self.groups) for p in (far, self.groups - far)]
        self.order = list(dict.fromkeys(near))

    def hand(self, source, target, owner, at, send_at, step, when):
        copy = pltpu.make_async_remote_copy(
            src_ref=source,
            dst_ref=target,
            send_sem=self.sems[0].at[(send_at, *at)],
            recv_sem=self.sems[1].at[(owner, *at)],
            device_id=(self.space, lax.rem(self.chan + self.groups + step, self.groups)),
            device_id_type=MESH,
        )
        pl.when(when)(copy.start)
        self.sent.append((copy, when))

    def begin(self, source, target, at):
        chan, last = self.chan, self.groups - 1
        self.hand(source, target, chan, at, chan, 1, chan < last)
        self.hand(source, target, chan, at, self.groups, -1, chan > 0)

    def take(self, target_of, at):
        chan, last = self.chan, self.groups - 1
        for p in self.order:
            owner = lax.rem(chan + self.groups - p, self.groups)
            target = target_of(owner)
            pltpu.make_async_remote_copy(
                src_ref=target,
                dst_ref=target,
                send_sem=self.sems[0].at[(owner, *at)],
                recv_sem=self.sems[1].at[(owner, *at)],
                device_id=(self.space, owner),
                device_id_type=MESH,
            ).wait_recv()
            up = (owner < chan) & (chan < last)
            down = (owner > chan) & (chan > 0)
            self.hand(target, target, owner, at, owner, 1, up)
            self.hand(target, target, owner, at, owner, -1, down)

    def finish(self):
        for copy, when in self.sent:
            pl.when(when)(copy.wait_send)


def gather_kernel(
    reach,
    geometry_ref,
    feature_ref,
    weight_ref,
    mix_ref,
    out_ref,
    state_ref,
    rows_ref,
    columns_ref,
    all_mix_ref,
    all_in_ref,
    landed,
    feature_v,
    weight_v,
    *sems,
):
    place = greet(reach, 2)
    space, chan, spatial, groups = place
    chan_sems, space_sems, near_sems, piece_sems, far_sems, pair_sems, own_sems = (
        sems[2 * i : 2 * i + 2] for i in range(7)
    )
    fetched = [
        pltpu.make_async_copy(feature_ref, feature_v, own_sems[0].at[0]),
        pltpu.make_async_copy(weight_ref.at[0], weight_v, own_sems[0].at[1]),
    ]
    for copy in fetched:
        copy.start()
    rows, _ = feature_ref.shape
    extent = out_ref.shape[1]
    blocks = geometry_ref.shape[0]

    shares = []
    for source, target in ((mix_ref, all_mix_ref), (weight_ref, all_in_ref)):
        part = target.shape[-2]
        mine = pl.ds(pl.multiple_of(space * part, part), part)
        if target is all_in_ref:
            held = source.at[pl.ds(1, LAYERS - 1), mine]
        else:
            held = source.at[:, mine]
        shares.append((held, target))
    leaving = []
    pieces, chunks = Line(place, piece_sems), Line(place, chan_sems)
    for kind, (held, target) in enumerate(shares):
        pieces.begin(held, target.at[space, chan], (kind,))
    rows_ref[:blocks] = geometry_ref[...]
    for offset in range(1, reach + 1):
        leaving.append(
            send(
                geometry_ref,
                rows_ref.at[pl.ds(offset * blocks, blocks)],
                near_sems,
                (offset - 1,),
                (lax.rem(space + spatial - offset, spatial), chan),
            )
        )
    for q in range(groups):
        chunks.begin(feature_ref.at[:, q * extent : (q + 1) * extent], landed.at[chan, q], (q,))
    kept = []
    for kind, (held, target) in enumerate(shares):
        kept.append(pltpu.make_async_copy(held, target.at[space, chan], own_sems[1].at[kind]))
        kept[-1].start()
    for copy in kept:
        copy.wait()
    for kind, (_, target) in enumerate(shares):
        pieces.take(lambda owner, target=target: target.at[space, owner], (kind,))
    far, paired = [], []
    partner = (space + 1 - 2 * lax.rem(space, 2), chan)
    for kind, (_, target) in enumerate(shares):
        for hop in range(1, spatial // 2):
            far.append(
                (
                    send(
                        target.at[space],
                        target.at[space],
                        far_sems,
                        (kind, hop - 1),
                        (lax.rem(space + 2 * hop, spatial), chan),
                    ),
                    kind,
                    hop,
                )
            )
        paired.append(send(target.at[space], target.at[space], pair_sems, (kind, 0), partner))
    for copy in fetched:
        copy.wait()
    for q in range(groups):
        chunks.take(lambda owner, q=q: landed.at[owner, q], (q,))
        total = 0.0
        for p in range(groups):
            source = lax.rem(chan + groups - p, groups)
            if p > 0:
                part = landed[source, q]
            else:
                part = feature_v[:, q * extent : (q + 1) * extent]
            columns = pl.ds(pl.multiple_of(source * rows, rows), rows)
            total = total + contract(weight_v[:, columns], part, 1, 0)
        out_ref[q] = total.T
        leaving += spread_block(out_ref, q, q, reach, groups, place, space_sems)
    own = pl.ds(pl.multiple_of(chan * extent, extent), extent)
    state_ref[chan] = feature_v[:, own]
    for p in range(1, groups):
        source = lax.rem(chan + groups - p, groups)
        state_ref[source] = landed[source, chan]
    for copy, kind, hop in far:
        copy.wait_recv()
        source = lax.rem(space + spatial - 2 * hop, spatial)
        target = shares[kind][1]
        paired.append(send(target.at[source], target.at[source], pair_sems, (kind, hop), partner))
    for copy in leaving + paired:
        copy.wait()
    for at in range(rows_ref.shape[0]):
        columns_ref[at] = rows_ref[at].T
    for copy, _, _ in far:
        copy.wait_send()
    pieces.finish()
    chunks.finish()


def mix_states(reach, layer, collected_ref, state_ref, mix_ref, back, sums, heard, place, back_sems, sum_sems):
    space, chan, spatial, groups = place
    order = list(range(1, groups)) + [0]
    copies, returning = [], {}
    for p in order:
        block = lax.rem(chan + p, groups)
        for offset in range(1, reach + 1):
            returning[offset, p] = send(
                collected_ref.at[offset * groups + block],
                back.at[offset - 1, p],
                back_sems,
                (offset - 1, p),
                (lax.rem(space + offset, spatial), chan),
            )
    telling = {}
    for p in order:
        block = lax.rem(chan + p, groups)
        total = collected_ref[block]
        for offset in range(1, reach + 1):
            returning[offset, p].wait_recv()
            total = total + back[offset - 1, p]
        sums[p] = total
        if p > 0:
            telling[p] = send(sums.at[p], heard.at[p - 1], sum_sems, (p - 1,), (space, block))
    copies += list(returning.values()) + list(telling.values())

    def weight(source):
        held = mix_ref[:, source, layer]
        return held.reshape(held.shape[0] * held.shape[1], held.shape[2])

    mixed = contract(weight(chan), sums[0], 1, 1)
    for p in range(1, groups):
        telling[p].wait_recv()
        mixed = mixed + contract(weight(lax.rem(chan + groups - p, groups)), heard[p - 1], 1, 1)
    old = state_ref[...]
    mixed = mixed.reshape(old.shape)
    return old + mixed / (1.0 + jnp.exp(-mixed)), copies


def middle_kernel(
    reach,
    layer,
    collected_ref,
    state_ref,
    mix_ref,
    in_ref,
    out_ref,
    new_ref,
    back,
    sums,
    heard,
    ready,
    *sems,
):
    place = greet(reach)
    space, chan, spatial, groups = place
    new_state, copies = mix_states(
        reach, layer, collected_ref, state_ref, mix_ref, back, sums, heard, place, sems[0:2], sems[2:4]
    )
    new_ref[...] = new_state
    flat = new_state.reshape(new_state.shape[0] * new_state.shape[1], new_state.shape[2])
    handing = {}
    for p in list(range(1, groups)) + [0]:
        target = lax.rem(chan + p, groups)
        held = in_ref[:, target, layer]
        held = held.reshape(held.shape[0] * held.shape[1], held.shape[2])
        mapped = contract(held, flat, 1, 0).T
        if p > 0:
            ready[p - 1] = mapped
            handing[p] = send(ready.at[p - 1], out_ref.at[chan], sems[4:6], (p - 1,), (space, target))
        else:
            out_ref[chan] = mapped
    leaving = spread_block(out_ref, chan, 0, reach, groups, place, sems[6:8])
    for p in range(1, groups):
        handing[p].wait_recv()
        block = lax.rem(chan + groups - p, groups)
        leaving += spread_block(out_ref, block, p, reach, groups, place, sems[6:8])
    for copy in copies + list(handing.values()):
        copy.wait_send()
    for copy in leaving:
        copy.wait()


def last_kernel(reach, layer, collected_ref, state_ref, mix_ref, out_ref, back, sums, heard, ready, *sems):
    place = greet(reach)
    space, chan, spatial, groups = place
    new_state, copies = mix_states(
        reach, layer, collected_ref, state_ref, mix_ref, back, sums, heard, place, sems[0:2], sems[2:4]
    )
    ready[...] = new_state
    extent = ready.shape[2]
    own = pl.ds(pl.multiple_of(chan * extent, extent), extent)
    handing = {}
    for p in range(1, groups):
        target = lax.rem(chan + p, groups)
        handing[p] = send(ready.at[target], out_ref.at[:, own], sems[4:6], (p - 1,), (space, target))
    out_ref[:, own] = ready[chan]
    for p in range(1, groups):
        handing[p].wait_recv()
    for copy in copies + list(handing.values()):
        copy.wait_send()


def remote_call(kernel, outs, scratch, pairs, collective, *operands, elsewhere=0):
    vmem = pl.BlockSpec(memory_space=pltpu.VMEM)
    sems = [pltpu.SemaphoreType.DMA(shape) for shape in pairs for _ in range(2)]
    return pl.pallas_call(
        kernel,
        out_shape=[jax.ShapeDtypeStruct(shape, jnp.float32) for shape in outs],
        in_specs=[vmem] * (len(operands) - elsewhere)
        + [pl.BlockSpec(memory_space=pl.ANY)] * elsewhere,
        out_specs=[vmem] * len(outs),
        scratch_shapes=[pltpu.VMEM(shape, jnp.float32) for shape in scratch] + sems,
        compiler_params=pltpu.CompilerParams(
            collective_id=collective, has_side_effects=True, vmem_limit_bytes=60 * 1024 * 1024
        ),
    )(*operands)


def exchanged_layers(geometry, features, in_weight, mix_weight, reach, pairs_of):
    spatial, groups = lax.axis_size("space"), lax.axis_size("chan")
    blocks, _, block_len = geometry.shape
    channels = features.shape[0]
    slots = (reach + 1) * blocks
    blocked = (slots, block_len, channels)
    held = (groups, channels, block_len)
    square = (block_len, channels)
    hops = spatial // 2
    mix_part = mix_weight.shape[1] // spatial
    in_part = in_weight.shape[1] // spatial
    mapped, state, rows, columns, all_mix, all_in = remote_call(
        functools.partial(gather_kernel, reach),
        [
            blocked,
            held,
            (slots, 8, block_len),
            (slots, block_len, 8),
            (spatial, groups, LAYERS, mix_part, mix_weight.shape[2]),
            (spatial, groups, LAYERS - 1, in_part, in_weight.shape[2]),
        ],
        [(groups, groups, channels, block_len), features.shape, in_weight.shape[1:]],
        [
            (groups + 1, groups),
            (reach, groups),
            (reach,),
            (groups + 1, 2),
            (2, hops - 1),
            (2, hops),
            (2,),
        ],
        0,
        geometry,
        features,
        in_weight,
        mix_weight,
        elsewhere=3,
    )
    scratch = [(reach, groups, *square), (groups, *square), (groups - 1, *square)]
    for layer in range(LAYERS - 1):
        collected = pairs_of(columns, rows, mapped, layer)
        mapped, state = remote_call(
            functools.partial(middle_kernel, reach, layer),
            [blocked, held],
            scratch + [(groups - 1, *square)],
            [(reach, groups), (groups - 1,), (groups - 1,), (reach, groups)],
            1,
            collected,
            state,
            all_mix,
            all_in,
        )
    collected = pairs_of(columns, rows, mapped, LAYERS - 1)
    (updated,) = remote_call(
        functools.partial(last_kernel, reach, LAYERS - 1),
        [features.shape],
        scratch + [held],
        [(reach, groups), (groups - 1,), (groups - 1,)],
        2,
        collected,
        state,
        all_mix,
    )
    return updated


def shards(positions, features, block_counts, pair_table, in_weight, filter_weight, mix_weight):
    spatial = lax.axis_size("space")
    reach_dev = spatial // 4
    own_index = lax.axis_index("space")
    blocks = block_counts.shape[0]
    atoms_dev = positions.shape[1]
    block_len = atoms_dev // blocks
    local_chan = features.shape[0]
    slot_total = (reach_dev + 1) * blocks
    valid = (
        (lax.broadcasted_iota(jnp.int32, (blocks, block_len), 1) < block_counts[:, None])
        .astype(jnp.float32)
        .reshape(1, atoms_dev)
    )
    geometry = jnp.concatenate([positions, valid, jnp.zeros((4, atoms_dev), jnp.float32)], axis=0)
    geometry = geometry.reshape(8, blocks, block_len).transpose(1, 0, 2)
    base = jnp.stack([own_index, jnp.int32(spatial)]).astype(jnp.int32)
    groups = lax.axis_size("chan")

    def pairs_of(columns, rows, mapped_blocks, layer):
        return pair_messages(
            base, pair_table, columns, rows, mapped_blocks, filter_weight[layer], blocks
        )

    whole_tiles = (
        local_chan % 128 == 0
        and block_len % 128 == 0
        and blocks == groups
        and spatial > 2 * reach_dev
        and spatial % 2 == 0
        and local_chan % (8 * spatial) == 0
    )
    if whole_tiles:
        return exchanged_layers(geometry, features, in_weight, mix_weight, reach_dev, pairs_of)
    fetched = [geometry]
    for offset in range(1, reach_dev + 1):
        fetched.append(shifted(geometry, "space", -offset))
    rows = jnp.concatenate(fetched, axis=0)
    columns = rows.transpose(0, 2, 1)
    state = features
    for layer in range(LAYERS):
        full_state = lax.all_gather(state, "chan", axis=0, tiled=True)
        mapped = lax.dot_general(
            full_state,
            in_weight[layer],
            (((0,), (1,)), ((), ())),
            precision=lax.Precision.HIGHEST,
            preferred_element_type=jnp.float32,
        )
        neighbours = [mapped]
        for offset in range(1, reach_dev + 1):
            neighbours.append(shifted(mapped, "space", -offset))
        mapped_blocks = jnp.concatenate(neighbours, axis=0).reshape(slot_total, block_len, local_chan)
        collected = pairs_of(columns, rows, mapped_blocks, layer).reshape(reach_dev + 1, atoms_dev, local_chan)
        received = collected[0]
        for offset in range(1, reach_dev + 1):
            received = received + shifted(collected[offset], "space", offset)
        mixed = lax.dot_general(
            mix_weight[layer],
            received,
            (((1,), (1,)), ((), ())),
            precision=lax.Precision.HIGHEST,
            preferred_element_type=jnp.float32,
        )
        own_mixed = lax.psum_scatter(mixed, "chan", scatter_dimension=0, tiled=True)
        state = state + jax.nn.silu(own_mixed)
    return state


def solution(mesh):
    placed = (
        P(None, "space"),
        P("chan", "space"),
        P("space"),
        P(None, "space"),
        P(None, "chan", None),
        P(None, None, "chan"),
        P(None, None, "chan"),
    )
    return jax.shard_map(
        shards, mesh=mesh, in_specs=placed, out_specs=P("chan", "space"), check_vma=False
    )
```

```python
import functools
import math

import jax
import jax.numpy as jnp
from jax import lax
from jax.experimental import pallas as pl
from jax.experimental.pallas import tpu as pltpu
from jax.sharding import PartitionSpec as P

K = 8
LAYERS = 2


cutoff_radius = 6.0
gamma_width = 1.5
spacing = cutoff_radius / (K - 1)


def shifted(block, axis, distance):
    devices = range(lax.axis_size(axis))
    route = [((i - distance) % len(devices), i) for i in devices]
    return lax.ppermute(block, axis, route)


def half_cosine(y):
    terms = [(-1) ** n * (math.pi / 2) ** (2 * n) / math.factorial(2 * n) for n in range(8)]
    total = jnp.full_like(y, terms[-1])
    for term in terms[-2::-1]:
        total = total * y + term
    return total


def split_halves(value):
    high = value.astype(jnp.bfloat16)
    low = (value - high.astype(jnp.float32)).astype(jnp.bfloat16)
    return high, low


def write_basis(columns, rows, weight, same, out):
    squared = 0.0
    for axis in range(3):
        offset = columns[:, axis : axis + 1] - rows[axis : axis + 1, :]
        squared = squared + offset * offset
    extent = squared.shape[0]
    limit = cutoff_radius * cutoff_radius
    near = jnp.minimum(squared, limit)
    distance = jnp.sqrt(near)
    root = half_cosine(near * (1.0 / limit))
    allowed = (columns[:, 3:4] * weight) * rows[3:4, :]
    diagonal = lax.broadcasted_iota(jnp.int32, (extent, extent), 0) == lax.broadcasted_iota(
        jnp.int32, (extent, extent), 1
    )
    dropped = (squared >= limit) | (diagonal & same)
    envelope = jnp.where(dropped, 0.0, root * root * allowed)
    middle = K // 2 - 1
    spread = distance - middle * spacing
    centre = jnp.exp(-gamma_width * spread * spread) * envelope
    slope = 2.0 * gamma_width * spacing
    up = jnp.exp(slope * distance)
    down = jnp.exp(-slope * distance)

    def put(k, value):
        high, low = split_halves(value)
        out[k * extent : (k + 1) * extent, :extent] = high
        out[k * extent : (k + 1) * extent, extent:] = low

    put(middle, centre)
    unit = gamma_width * spacing * spacing
    value = centre
    for k in range(middle + 1, K):
        value = value * (up * math.exp(-unit * (2 * k - 1)))
        put(k, value)
    value = centre
    for k in range(middle - 1, -1, -1):
        value = value * (down * math.exp(unit * (2 * k + 1)))
        put(k, value)


def pair_kernel(
    blocks,
    base_ref,
    table_ref,
    columns_ref,
    rows_ref,
    mapped_ref,
    filter_ref,
    turned_ref,
    out_ref,
    count_s,
    to_s,
    from_s,
    weight_s,
    operand_v,
    scaled_v,
    other_v,
    basis_a,
    basis_b,
):
    slots, extent, channels = mapped_ref.shape
    spatial = base_ref[1]
    own = base_ref[0]

    def clear(i, carry):
        count_s[i] = 0
        return carry

    lax.fori_loop(0, blocks * slots, clear, 0)

    def tally(p, carry):
        first = table_ref[0, p] - own * blocks
        second = table_ref[1, p]
        holder = second // blocks
        ahead = holder - own
        ahead = jnp.where(ahead < 0, ahead + spatial, ahead)
        second = ahead * blocks + (second - holder * blocks)
        swap = second < first
        at = jnp.where(swap, second, first) * slots + jnp.where(swap, first, second)
        count_s[at] = count_s[at] + table_ref[2, p]
        return carry

    lax.fori_loop(0, table_ref.shape[1], tally, 0)

    def list_row(first, n):
        def list_one(second, n):
            many = count_s[first * slots + second]
            to_s[n] = first
            from_s[n] = second
            weight_s[n] = many.astype(jnp.float32)
            return n + (many > 0).astype(jnp.int32)

        return lax.fori_loop(first, slots, list_one, n)

    total = lax.fori_loop(0, blocks, list_row, 0)
    for extra in range(3):
        to_s[total + extra] = 0
        from_s[total + extra] = 0
        weight_s[total + extra] = 0.0

    for slot in range(slots):
        high, low = split_halves(mapped_ref[slot])
        for part in range(2):
            operand_v[slot, part * extent : (part + 1) * extent, :channels] = high
            operand_v[slot, part * extent : (part + 1) * extent, channels:] = low
    for slot in range(blocks):
        turned = mapped_ref[slot].T
        for k in range(K):
            high, low = split_halves(turned * turned_ref[:, k : k + 1])
            scaled_v[slot, :channels, k * extent : (k + 1) * extent] = high
            scaled_v[slot, channels:, k * extent : (k + 1) * extent] = low
    out_ref[...] = jnp.zeros_like(out_ref)
    other_v[...] = jnp.zeros_like(other_v)

    def build(task, basis):
        to, source = to_s[task], from_s[task]
        write_basis(columns_ref[to], rows_ref[source], weight_s[task], to == source, basis)

    def spend(task, basis):
        to, source = to_s[task], from_s[task]
        product = jnp.dot(basis[...], operand_v[source], preferred_element_type=jnp.float32)
        summed = 0.0
        for k in range(K):
            part = product[k * extent : (k + 1) * extent]
            summed = summed + filter_ref[k : k + 1, :] * (part[:, :channels] + part[:, channels:])
        out_ref[to] = out_ref[to] + summed
        both = jnp.dot(scaled_v[to], basis[...], preferred_element_type=jnp.float32)
        back = both[:channels] + both[channels:]
        back = back[:, :extent] + back[:, extent:]
        other_v[source] = other_v[source] + back * jnp.where(to == source, 0.0, 1.0)

    build(0, basis_a)

    def step(turn, carry):
        task = 2 * turn
        build(task + 1, basis_b)
        spend(task, basis_a)
        build(task + 2, basis_a)
        spend(task + 1, basis_b)
        return carry

    lax.fori_loop(0, (total + 1) // 2, step, 0)
    for slot in range(slots):
        out_ref[slot] = out_ref[slot] + other_v[slot].T


def pair_messages(base, table, columns, rows, mapped, filters, blocks, interpret=False):
    slots, extent, channels = mapped.shape
    tasks = blocks * slots + 8
    smem = pl.BlockSpec(memory_space=pltpu.SMEM)
    vmem = pl.BlockSpec(memory_space=pltpu.VMEM)
    return pl.pallas_call(
        functools.partial(pair_kernel, blocks),
        out_shape=jax.ShapeDtypeStruct(mapped.shape, jnp.float32),
        in_specs=[smem, smem, vmem, vmem, vmem, vmem, vmem],
        out_specs=vmem,
        scratch_shapes=[
            pltpu.SMEM((blocks * slots,), jnp.int32),
            pltpu.SMEM((tasks,), jnp.int32),
            pltpu.SMEM((tasks,), jnp.int32),
            pltpu.SMEM((tasks,), jnp.float32),
            pltpu.VMEM((slots, 2 * extent, 2 * channels), jnp.bfloat16),
            pltpu.VMEM((blocks, 2 * channels, K * extent), jnp.bfloat16),
            pltpu.VMEM((slots, channels, extent), jnp.float32),
            pltpu.VMEM((K * extent, 2 * extent), jnp.bfloat16),
            pltpu.VMEM((K * extent, 2 * extent), jnp.bfloat16),
        ],
        compiler_params=pltpu.CompilerParams(vmem_limit_bytes=48 * 1024 * 1024),
        interpret=interpret,
    )(base, table, columns, rows, mapped, filters, filters.T)


HIGHEST = lax.Precision.HIGHEST
MESH = pl.DeviceIdType.MESH


def contract(left, right, left_dim, right_dim):
    return lax.dot_general(
        left,
        right,
        (((left_dim,), (right_dim,)), ((), ())),
        precision=HIGHEST,
        preferred_element_type=jnp.float32,
    )


def greet(reach, stride=None):
    space, chan = lax.axis_index("space"), lax.axis_index("chan")
    spatial, groups = lax.axis_size("space"), lax.axis_size("chan")
    barrier = pltpu.get_barrier_semaphore()
    partners = [(space, lax.rem(chan + p, groups)) for p in range(1, groups)]
    offsets = set(range(1, reach + 1)) | {spatial - offset for offset in range(1, reach + 1)}
    if stride is not None:
        offsets |= set(range(stride, spatial, stride))
    for offset in sorted(offsets):
        partners.append((lax.rem(space + offset, spatial), chan))
    for partner in partners:
        pl.semaphore_signal(barrier, inc=1, device_id=partner, device_id_type=MESH)
    pl.semaphore_wait(barrier, len(partners))
    return space, chan, spatial, groups


def send(source, target, sems, at, device):
    copy = pltpu.make_async_remote_copy(
        src_ref=source,
        dst_ref=target,
        send_sem=sems[0].at[at],
        recv_sem=sems[1].at[at],
        device_id=device,
        device_id_type=MESH,
    )
    copy.start()
    return copy


def spread_block(out_ref, block, p, reach, blocks, place, sems):
    space, chan, spatial, groups = place
    copies = []
    for offset in range(1, reach + 1):
        copies.append(
            send(
                out_ref.at[block],
                out_ref.at[offset * blocks + block],
                sems,
                (offset - 1, p),
                (lax.rem(space + spatial - offset, spatial), chan),
            )
        )
    return copies


def gather_kernel(
    reach,
    geometry_ref,
    feature_ref,
    weight_ref,
    mix_ref,
    out_ref,
    state_ref,
    rows_ref,
    columns_ref,
    all_mix_ref,
    all_in_ref,
    landed,
    feature_v,
    weight_v,
    *sems,
):
    place = greet(reach, 2)
    space, chan, spatial, groups = place
    chan_sems, space_sems, near_sems, piece_sems, far_sems, pair_sems, own_sems = (
        sems[2 * i : 2 * i + 2] for i in range(7)
    )
    fetched = [
        pltpu.make_async_copy(feature_ref, feature_v, own_sems[0].at[0]),
        pltpu.make_async_copy(weight_ref.at[0], weight_v, own_sems[0].at[1]),
    ]
    for copy in fetched:
        copy.start()
    rows, _ = feature_ref.shape
    extent = out_ref.shape[1]
    blocks = geometry_ref.shape[0]

    shares = []
    for source, target in ((mix_ref, all_mix_ref), (weight_ref, all_in_ref)):
        part = target.shape[-2]
        mine = pl.ds(pl.multiple_of(space * part, part), part)
        first_layer = 1 if target is all_in_ref else 0
        held = source.at[pl.ds(first_layer, LAYERS - 1), mine]
        shares.append((held, target))
    pieces, leaving = [], []
    for p in range(1, groups):
        for kind, (held, target) in enumerate(shares):
            pieces.append(
                send(
                    held,
                    target.at[space, chan],
                    piece_sems,
                    (kind, p - 1),
                    (space, lax.rem(chan + p, groups)),
                )
            )
    rows_ref[:blocks] = geometry_ref[...]
    for offset in range(1, reach + 1):
        leaving.append(
            send(
                geometry_ref,
                rows_ref.at[pl.ds(offset * blocks, blocks)],
                near_sems,
                (offset - 1,),
                (lax.rem(space + spatial - offset, spatial), chan),
            )
        )
    arriving = {}

    def tell(q):
        for p in range(1, groups):
            arriving[p, q] = send(
                feature_ref.at[:, q * extent : (q + 1) * extent],
                landed.at[p - 1, q],
                chan_sems,
                (p - 1, q),
                (space, lax.rem(chan + p, groups)),
            )

    tell(0)
    kept = []
    for kind, (held, target) in enumerate(shares):
        kept.append(pltpu.make_async_copy(held, target.at[space, chan], own_sems[1].at[kind]))
        kept[-1].start()
    for copy in kept:
        copy.wait()
    for copy in pieces:
        copy.wait_recv()
    far, paired = [], []
    partner = (space + 1 - 2 * lax.rem(space, 2), chan)
    for kind, (_, target) in enumerate(shares):
        for hop in range(1, spatial // 2):
            far.append(
                (
                    send(
                        target.at[space],
                        target.at[space],
                        far_sems,
                        (kind, hop - 1),
                        (lax.rem(space + 2 * hop, spatial), chan),
                    ),
                    kind,
                    hop,
                )
            )
        paired.append(send(target.at[space], target.at[space], pair_sems, (kind, 0), partner))
    for q in range(1, groups):
        tell(q)
    for copy in fetched:
        copy.wait()
    for q in range(groups):
        total = 0.0
        for p in range(groups):
            if p > 0:
                arriving[p, q].wait_recv()
                part = landed[p - 1, q]
            else:
                part = feature_v[:, q * extent : (q + 1) * extent]
            source = lax.rem(chan + groups - p, groups)
            columns = pl.ds(pl.multiple_of(source * rows, rows), rows)
            total = total + contract(weight_v[:, columns], part, 1, 0)
        out_ref[q] = total.T
        leaving += spread_block(out_ref, q, q, reach, groups, place, space_sems)
    own = pl.ds(pl.multiple_of(chan * extent, extent), extent)
    state_ref[chan] = feature_v[:, own]
    for p in range(1, groups):
        state_ref[lax.rem(chan + groups - p, groups)] = landed[p - 1, chan]
    for copy, kind, hop in far:
        copy.wait_recv()
        source = lax.rem(space + spatial - 2 * hop, spatial)
        target = shares[kind][1]
        paired.append(send(target.at[source], target.at[source], pair_sems, (kind, hop), partner))
    for copy in leaving + paired:
        copy.wait()
    for at in range(rows_ref.shape[0]):
        columns_ref[at] = rows_ref[at].T
    for copy in list(arriving.values()) + pieces + [copy for copy, _, _ in far]:
        copy.wait_send()


def mix_states(reach, layer, collected_ref, state_ref, mix_ref, back, sums, heard, place, back_sems, sum_sems):
    space, chan, spatial, groups = place
    order = list(range(1, groups)) + [0]
    copies, returning = [], {}
    for p in order:
        block = lax.rem(chan + p, groups)
        for offset in range(1, reach + 1):
            returning[offset, p] = send(
                collected_ref.at[offset * groups + block],
                back.at[offset - 1, p],
                back_sems,
                (offset - 1, p),
                (lax.rem(space + offset, spatial), chan),
            )
    telling = {}
    for p in order:
        block = lax.rem(chan + p, groups)
        total = collected_ref[block]
        for offset in range(1, reach + 1):
            returning[offset, p].wait_recv()
            total = total + back[offset - 1, p]
        sums[p] = total
        if p > 0:
            telling[p] = send(sums.at[p], heard.at[p - 1], sum_sems, (p - 1,), (space, block))
    copies += list(returning.values()) + list(telling.values())

    def weight(source):
        held = mix_ref[:, source, layer]
        return held.reshape(held.shape[0] * held.shape[1], held.shape[2])

    mixed = contract(weight(chan), sums[0], 1, 1)
    for p in range(1, groups):
        telling[p].wait_recv()
        mixed = mixed + contract(weight(lax.rem(chan + groups - p, groups)), heard[p - 1], 1, 1)
    old = state_ref[...]
    mixed = mixed.reshape(old.shape)
    return old + mixed / (1.0 + jnp.exp(-mixed)), copies


def middle_kernel(
    reach,
    layer,
    collected_ref,
    state_ref,
    mix_ref,
    in_ref,
    out_ref,
    new_ref,
    back,
    sums,
    heard,
    ready,
    *sems,
):
    place = greet(reach)
    space, chan, spatial, groups = place
    new_state, copies = mix_states(
        reach, layer, collected_ref, state_ref, mix_ref, back, sums, heard, place, sems[0:2], sems[2:4]
    )
    new_ref[...] = new_state
    flat = new_state.reshape(new_state.shape[0] * new_state.shape[1], new_state.shape[2])
    handing = {}
    for p in list(range(1, groups)) + [0]:
        target = lax.rem(chan + p, groups)
        held = in_ref[:, target, layer]
        held = held.reshape(held.shape[0] * held.shape[1], held.shape[2])
        mapped = contract(held, flat, 1, 0).T
        if p > 0:
            ready[p - 1] = mapped
            handing[p] = send(ready.at[p - 1], out_ref.at[chan], sems[4:6], (p - 1,), (space, target))
        else:
            out_ref[chan] = mapped
    leaving = spread_block(out_ref, chan, 0, reach, groups, place, sems[6:8])
    for p in range(1, groups):
        handing[p].wait_recv()
        block = lax.rem(chan + groups - p, groups)
        leaving += spread_block(out_ref, block, p, reach, groups, place, sems[6:8])
    for copy in copies + list(handing.values()):
        copy.wait_send()
    for copy in leaving:
        copy.wait()


def last_kernel(reach, layer, collected_ref, state_ref, mix_ref, out_ref, back, sums, heard, ready, *sems):
    place = greet(reach)
    space, chan, spatial, groups = place
    new_state, copies = mix_states(
        reach, layer, collected_ref, state_ref, mix_ref, back, sums, heard, place, sems[0:2], sems[2:4]
    )
    ready[...] = new_state
    extent = ready.shape[2]
    own = pl.ds(pl.multiple_of(chan * extent, extent), extent)
    handing = {}
    for p in range(1, groups):
        target = lax.rem(chan + p, groups)
        handing[p] = send(ready.at[target], out_ref.at[:, own], sems[4:6], (p - 1,), (space, target))
    out_ref[:, own] = ready[chan]
    for p in range(1, groups):
        handing[p].wait_recv()
    for copy in copies + list(handing.values()):
        copy.wait_send()


def remote_call(kernel, outs, scratch, pairs, collective, *operands, elsewhere=0, grant=40):
    vmem = pl.BlockSpec(memory_space=pltpu.VMEM)
    sems = [pltpu.SemaphoreType.DMA(shape) for shape in pairs for _ in range(2)]
    return pl.pallas_call(
        kernel,
        out_shape=[jax.ShapeDtypeStruct(shape, jnp.float32) for shape in outs],
        in_specs=[vmem] * (len(operands) - elsewhere)
        + [pl.BlockSpec(memory_space=pl.ANY)] * elsewhere,
        out_specs=[vmem] * len(outs),
        scratch_shapes=[pltpu.VMEM(shape, jnp.float32) for shape in scratch] + sems,
        compiler_params=pltpu.CompilerParams(
            collective_id=collective, has_side_effects=True, vmem_limit_bytes=grant * 1024 * 1024
        ),
    )(*operands)


def all_pieces(local):
    spatial = lax.axis_size("space")
    part = local.shape[0] // spatial
    share = lax.dynamic_slice_in_dim(local, lax.axis_index("space") * part, part, 0)
    gathered = lax.all_gather(share, ("space", "chan"), axis=0, tiled=False)
    return gathered.reshape(spatial, lax.axis_size("chan"), 1, part, local.shape[1])


def exchanged_layers(geometry, features, in_weight, mix_weight, reach, pairs_of):
    spatial, groups = lax.axis_size("space"), lax.axis_size("chan")
    blocks, _, block_len = geometry.shape
    channels = features.shape[0]
    slots = (reach + 1) * blocks
    blocked = (slots, block_len, channels)
    held = (groups, channels, block_len)
    square = (block_len, channels)
    hops = spatial // 2
    mix_part = mix_weight.shape[1] // spatial
    in_part = in_weight.shape[1] // spatial
    last_mix = all_pieces(mix_weight[LAYERS - 1])
    mapped, state, rows, columns, all_mix, all_in = remote_call(
        functools.partial(gather_kernel, reach),
        [
            blocked,
            held,
            (slots, 8, block_len),
            (slots, block_len, 8),
            (spatial, groups, LAYERS - 1, mix_part, mix_weight.shape[2]),
            (spatial, groups, LAYERS - 1, in_part, in_weight.shape[2]),
        ],
        [(groups - 1, groups, channels, block_len), features.shape, in_weight.shape[1:]],
        [
            (groups - 1, groups),
            (reach, groups),
            (reach,),
            (2, groups - 1),
            (2, hops - 1),
            (2, hops),
            (2,),
        ],
        0,
        geometry,
        features,
        in_weight,
        mix_weight,
        elsewhere=3,
        grant=60,
    )
    scratch = [(reach, groups, *square), (groups, *square), (groups - 1, *square)]
    for layer in range(LAYERS - 1):
        collected = pairs_of(columns, rows, mapped, layer)
        mapped, state = remote_call(
            functools.partial(middle_kernel, reach, layer),
            [blocked, held],
            scratch + [(groups - 1, *square)],
            [(reach, groups), (groups - 1,), (groups - 1,), (reach, groups)],
            1,
            collected,
            state,
            all_mix,
            all_in,
        )
    collected = pairs_of(columns, rows, mapped, LAYERS - 1)
    (updated,) = remote_call(
        functools.partial(last_kernel, reach, 0),
        [features.shape],
        scratch + [held],
        [(reach, groups), (groups - 1,), (groups - 1,)],
        2,
        collected,
        state,
        last_mix,
    )
    return updated


def shards(positions, features, block_counts, pair_table, in_weight, filter_weight, mix_weight):
    spatial = lax.axis_size("space")
    reach_dev = spatial // 4
    own_index = lax.axis_index("space")
    blocks = block_counts.shape[0]
    atoms_dev = positions.shape[1]
    block_len = atoms_dev // blocks
    local_chan = features.shape[0]
    slot_total = (reach_dev + 1) * blocks
    valid = (
        (lax.broadcasted_iota(jnp.int32, (blocks, block_len), 1) < block_counts[:, None])
        .astype(jnp.float32)
        .reshape(1, atoms_dev)
    )
    geometry = jnp.concatenate([positions, valid, jnp.zeros((4, atoms_dev), jnp.float32)], axis=0)
    geometry = geometry.reshape(8, blocks, block_len).transpose(1, 0, 2)
    base = jnp.stack([own_index, jnp.int32(spatial)]).astype(jnp.int32)
    groups = lax.axis_size("chan")

    def pairs_of(columns, rows, mapped_blocks, layer):
        return pair_messages(
            base, pair_table, columns, rows, mapped_blocks, filter_weight[layer], blocks
        )

    whole_tiles = (
        local_chan % 128 == 0
        and block_len % 128 == 0
        and blocks == groups
        and spatial > 2 * reach_dev
        and spatial % 2 == 0
        and local_chan % (8 * spatial) == 0
    )
    if whole_tiles:
        return exchanged_layers(geometry, features, in_weight, mix_weight, reach_dev, pairs_of)
    fetched = [geometry]
    for offset in range(1, reach_dev + 1):
        fetched.append(shifted(geometry, "space", -offset))
    rows = jnp.concatenate(fetched, axis=0)
    columns = rows.transpose(0, 2, 1)
    state = features
    for layer in range(LAYERS):
        full_state = lax.all_gather(state, "chan", axis=0, tiled=True)
        mapped = lax.dot_general(
            full_state,
            in_weight[layer],
            (((0,), (1,)), ((), ())),
            precision=lax.Precision.HIGHEST,
            preferred_element_type=jnp.float32,
        )
        neighbours = [mapped]
        for offset in range(1, reach_dev + 1):
            neighbours.append(shifted(mapped, "space", -offset))
        mapped_blocks = jnp.concatenate(neighbours, axis=0).reshape(slot_total, block_len, local_chan)
        collected = pairs_of(columns, rows, mapped_blocks, layer).reshape(reach_dev + 1, atoms_dev, local_chan)
        received = collected[0]
        for offset in range(1, reach_dev + 1):
            received = received + shifted(collected[offset], "space", offset)
        mixed = lax.dot_general(
            mix_weight[layer],
            received,
            (((1,), (1,)), ((), ())),
            precision=lax.Precision.HIGHEST,
            preferred_element_type=jnp.float32,
        )
        own_mixed = lax.psum_scatter(mixed, "chan", scatter_dimension=0, tiled=True)
        state = state + jax.nn.silu(own_mixed)
    return state


def solution(mesh):
    placed = (
        P(None, "space"),
        P("chan", "space"),
        P("space"),
        P(None, "space"),
        P(None, "chan", None),
        P(None, None, "chan"),
        P(None, None, "chan"),
    )
    return jax.shard_map(
        shards, mesh=mesh, in_specs=placed, out_specs=P("chan", "space"), check_vma=False
    )
```

```python
import functools
import math

import jax
import jax.numpy as jnp
from jax import lax
from jax.experimental import pallas as pl
from jax.experimental.pallas import tpu as pltpu
from jax.sharding import PartitionSpec as P

K = 8
LAYERS = 2


cutoff_radius = 6.0
gamma_width = 1.5
spacing = cutoff_radius / (K - 1)


def shifted(block, axis, distance):
    devices = range(lax.axis_size(axis))
    route = [((i - distance) % len(devices), i) for i in devices]
    return lax.ppermute(block, axis, route)


def half_cosine(y):
    terms = [(-1) ** n * (math.pi / 2) ** (2 * n) / math.factorial(2 * n) for n in range(8)]
    total = jnp.full_like(y, terms[-1])
    for term in terms[-2::-1]:
        total = total * y + term
    return total


def split_halves(value):
    high = value.astype(jnp.bfloat16)
    low = (value - high.astype(jnp.float32)).astype(jnp.bfloat16)
    return high, low


def write_basis(columns, rows, weight, same, out):
    squared = 0.0
    for axis in range(3):
        offset = columns[:, axis : axis + 1] - rows[axis : axis + 1, :]
        squared = squared + offset * offset
    extent = squared.shape[0]
    limit = cutoff_radius * cutoff_radius
    near = jnp.minimum(squared, limit)
    distance = jnp.sqrt(near)
    root = half_cosine(near * (1.0 / limit))
    allowed = (columns[:, 3:4] * weight) * rows[3:4, :]
    diagonal = lax.broadcasted_iota(jnp.int32, (extent, extent), 0) == lax.broadcasted_iota(
        jnp.int32, (extent, extent), 1
    )
    dropped = (squared >= limit) | (diagonal & same)
    envelope = jnp.where(dropped, 0.0, root * root * allowed)
    middle = K // 2 - 1
    spread = distance - middle * spacing
    centre = jnp.exp(-gamma_width * spread * spread) * envelope
    slope = 2.0 * gamma_width * spacing
    up = jnp.exp(slope * distance)
    down = jnp.exp(-slope * distance)

    def put(k, value):
        high, low = split_halves(value)
        out[k * extent : (k + 1) * extent, :extent] = high
        out[k * extent : (k + 1) * extent, extent:] = low

    put(middle, centre)
    unit = gamma_width * spacing * spacing
    value = centre
    for k in range(middle + 1, K):
        value = value * (up * math.exp(-unit * (2 * k - 1)))
        put(k, value)
    value = centre
    for k in range(middle - 1, -1, -1):
        value = value * (down * math.exp(unit * (2 * k + 1)))
        put(k, value)


def pair_kernel(
    blocks,
    base_ref,
    table_ref,
    columns_ref,
    rows_ref,
    mapped_ref,
    filter_ref,
    turned_ref,
    out_ref,
    count_s,
    to_s,
    from_s,
    weight_s,
    operand_v,
    scaled_v,
    other_v,
    basis_a,
    basis_b,
):
    slots, extent, channels = mapped_ref.shape
    spatial = base_ref[1]
    own = base_ref[0]

    def clear(i, carry):
        count_s[i] = 0
        return carry

    lax.fori_loop(0, blocks * slots, clear, 0)

    def tally(p, carry):
        first = table_ref[0, p] - own * blocks
        second = table_ref[1, p]
        holder = second // blocks
        ahead = holder - own
        ahead = jnp.where(ahead < 0, ahead + spatial, ahead)
        second = ahead * blocks + (second - holder * blocks)
        swap = second < first
        at = jnp.where(swap, second, first) * slots + jnp.where(swap, first, second)
        count_s[at] = count_s[at] + table_ref[2, p]
        return carry

    lax.fori_loop(0, table_ref.shape[1], tally, 0)

    def list_row(first, n):
        def list_one(second, n):
            many = count_s[first * slots + second]
            to_s[n] = first
            from_s[n] = second
            weight_s[n] = many.astype(jnp.float32)
            return n + (many > 0).astype(jnp.int32)

        return lax.fori_loop(first, slots, list_one, n)

    total = lax.fori_loop(0, blocks, list_row, 0)
    for extra in range(3):
        to_s[total + extra] = 0
        from_s[total + extra] = 0
        weight_s[total + extra] = 0.0

    for slot in range(slots):
        high, low = split_halves(mapped_ref[slot])
        for part in range(2):
            operand_v[slot, part * extent : (part + 1) * extent, :channels] = high
            operand_v[slot, part * extent : (part + 1) * extent, channels:] = low
    for slot in range(blocks):
        turned = mapped_ref[slot].T
        for k in range(K):
            high, low = split_halves(turned * turned_ref[:, k : k + 1])
            scaled_v[slot, :channels, k * extent : (k + 1) * extent] = high
            scaled_v[slot, channels:, k * extent : (k + 1) * extent] = low
    out_ref[...] = jnp.zeros_like(out_ref)
    other_v[...] = jnp.zeros_like(other_v)

    def build(task, basis):
        to, source = to_s[task], from_s[task]
        write_basis(columns_ref[to], rows_ref[source], weight_s[task], to == source, basis)

    def spend(task, basis):
        to, source = to_s[task], from_s[task]
        product = jnp.dot(basis[...], operand_v[source], preferred_element_type=jnp.float32)
        summed = 0.0
        for k in range(K):
            part = product[k * extent : (k + 1) * extent]
            summed = summed + filter_ref[k : k + 1, :] * (part[:, :channels] + part[:, channels:])
        out_ref[to] = out_ref[to] + summed
        both = jnp.dot(scaled_v[to], basis[...], preferred_element_type=jnp.float32)
        back = both[:channels] + both[channels:]
        back = back[:, :extent] + back[:, extent:]
        other_v[source] = other_v[source] + back * jnp.where(to == source, 0.0, 1.0)

    build(0, basis_a)

    def step(turn, carry):
        task = 2 * turn
        build(task + 1, basis_b)
        spend(task, basis_a)
        build(task + 2, basis_a)
        spend(task + 1, basis_b)
        return carry

    lax.fori_loop(0, (total + 1) // 2, step, 0)
    for slot in range(slots):
        out_ref[slot] = out_ref[slot] + other_v[slot].T


def pair_messages(base, table, columns, rows, mapped, filters, blocks, interpret=False):
    slots, extent, channels = mapped.shape
    tasks = blocks * slots + 8
    smem = pl.BlockSpec(memory_space=pltpu.SMEM)
    vmem = pl.BlockSpec(memory_space=pltpu.VMEM)
    return pl.pallas_call(
        functools.partial(pair_kernel, blocks),
        out_shape=jax.ShapeDtypeStruct(mapped.shape, jnp.float32),
        in_specs=[smem, smem, vmem, vmem, vmem, vmem, vmem],
        out_specs=vmem,
        scratch_shapes=[
            pltpu.SMEM((blocks * slots,), jnp.int32),
            pltpu.SMEM((tasks,), jnp.int32),
            pltpu.SMEM((tasks,), jnp.int32),
            pltpu.SMEM((tasks,), jnp.float32),
            pltpu.VMEM((slots, 2 * extent, 2 * channels), jnp.bfloat16),
            pltpu.VMEM((blocks, 2 * channels, K * extent), jnp.bfloat16),
            pltpu.VMEM((slots, channels, extent), jnp.float32),
            pltpu.VMEM((K * extent, 2 * extent), jnp.bfloat16),
            pltpu.VMEM((K * extent, 2 * extent), jnp.bfloat16),
        ],
        compiler_params=pltpu.CompilerParams(vmem_limit_bytes=48 * 1024 * 1024),
        interpret=interpret,
    )(base, table, columns, rows, mapped, filters, filters.T)


MESH = pl.DeviceIdType.MESH


def contract(left, right, left_dim, right_dim):
    left, right = split_halves(left), split_halves(right)
    total = 0.0
    for one, other in ((0, 0), (0, 1), (1, 0)):
        total = total + lax.dot_general(
            left[one],
            right[other],
            (((left_dim,), (right_dim,)), ((), ())),
            preferred_element_type=jnp.float32,
        )
    return total


def greet(reach, stride=None):
    space, chan = lax.axis_index("space"), lax.axis_index("chan")
    spatial, groups = lax.axis_size("space"), lax.axis_size("chan")
    barrier = pltpu.get_barrier_semaphore()
    partners = [(space, lax.rem(chan + p, groups)) for p in range(1, groups)]
    offsets = set(range(1, reach + 1)) | {spatial - offset for offset in range(1, reach + 1)}
    if stride is not None:
        offsets |= set(range(stride, spatial, stride))
    for offset in sorted(offsets):
        partners.append((lax.rem(space + offset, spatial), chan))
    for partner in partners:
        pl.semaphore_signal(barrier, inc=1, device_id=partner, device_id_type=MESH)
    pl.semaphore_wait(barrier, len(partners))
    return space, chan, spatial, groups


def send(source, target, sems, at, device):
    copy = pltpu.make_async_remote_copy(
        src_ref=source,
        dst_ref=target,
        send_sem=sems[0].at[at],
        recv_sem=sems[1].at[at],
        device_id=device,
        device_id_type=MESH,
    )
    copy.start()
    return copy


def spread_block(out_ref, block, p, reach, blocks, place, sems):
    space, chan, spatial, groups = place
    copies = {}
    for offset in range(1, reach + 1):
        copies[offset] = pltpu.make_async_remote_copy(
            src_ref=out_ref.at[block],
            dst_ref=out_ref.at[offset * blocks + block],
            send_sem=sems[0].at[offset - 1, p],
            recv_sem=sems[1].at[offset - 1, p],
            device_id=(lax.rem(space + spatial - offset, spatial), chan),
            device_id_type=MESH,
        )
        if offset == 1 and reach > 1:
            pl.when(lax.rem(space, 2) == 1)(copies[offset].start)
        else:
            copies[offset].start()
    return [(block, p, copies)]


def finish_blocks(out_ref, leaving, reach, blocks, place, sems):
    space, chan, spatial, groups = place
    for block, p, copies in leaving:
        if reach > 1:
            copies[2].wait_recv()
            onward = pltpu.make_async_remote_copy(
                src_ref=out_ref.at[2 * blocks + block],
                dst_ref=out_ref.at[blocks + block],
                send_sem=sems[0].at[0, p],
                recv_sem=sems[1].at[0, p],
                device_id=(lax.rem(space + 1, spatial), chan),
                device_id_type=MESH,
            )
            pl.when(lax.rem(space, 2) == 0)(onward.start)
    for block, p, copies in leaving:
        for offset, copy in copies.items():
            if offset != 2:
                copy.wait_recv()
            copy.wait_send()


def gather_kernel(
    reach,
    geometry_ref,
    feature_ref,
    weight_ref,
    mix_ref,
    out_ref,
    state_ref,
    rows_ref,
    columns_ref,
    all_mix_ref,
    all_in_ref,
    landed,
    feature_v,
    weight_v,
    *sems,
):
    place = greet(reach, 2)
    space, chan, spatial, groups = place
    chan_sems, space_sems, near_sems, piece_sems, far_sems, pair_sems, own_sems = (
        sems[2 * i : 2 * i + 2] for i in range(7)
    )
    fetched = [
        pltpu.make_async_copy(feature_ref, feature_v, own_sems[0].at[0]),
        pltpu.make_async_copy(weight_ref.at[0], weight_v, own_sems[0].at[1]),
    ]
    for copy in fetched:
        copy.start()
    rows, _ = feature_ref.shape
    extent = out_ref.shape[1]
    blocks = geometry_ref.shape[0]

    shares = []
    for source, target in ((mix_ref, all_mix_ref), (weight_ref, all_in_ref)):
        part = target.shape[-2]
        mine = pl.ds(pl.multiple_of(space * part, part), part)
        if target is all_in_ref:
            held = source.at[pl.ds(1, LAYERS - 1), mine]
        else:
            held = source.at[:, mine]
        shares.append((held, target))
    pieces, leaving, shifts = [], [], []
    for p in range(1, groups):
        for kind, (held, target) in enumerate(shares):
            pieces.append(
                send(
                    held,
                    target.at[space, chan],
                    piece_sems,
                    (kind, p - 1),
                    (space, lax.rem(chan + p, groups)),
                )
            )
    rows_ref[:blocks] = geometry_ref[...]
    for offset in range(1, reach + 1):
        shifts.append(
            send(
                geometry_ref,
                rows_ref.at[pl.ds(offset * blocks, blocks)],
                near_sems,
                (offset - 1,),
                (lax.rem(space + spatial - offset, spatial), chan),
            )
        )
    arriving = {}

    def tell(q):
        for p in range(1, groups):
            arriving[p, q] = send(
                feature_ref.at[:, q * extent : (q + 1) * extent],
                landed.at[p - 1, q],
                chan_sems,
                (p - 1, q),
                (space, lax.rem(chan + p, groups)),
            )

    tell(0)
    kept = []
    for kind, (held, target) in enumerate(shares):
        kept.append(pltpu.make_async_copy(held, target.at[space, chan], own_sems[1].at[kind]))
        kept[-1].start()
    for copy in kept:
        copy.wait()
    for copy in pieces:
        copy.wait_recv()
    far, paired = [], []
    partner = (space + 1 - 2 * lax.rem(space, 2), chan)
    for kind, (_, target) in enumerate(shares):
        for hop in range(1, spatial // 2):
            far.append(
                (
                    send(
                        target.at[space],
                        target.at[space],
                        far_sems,
                        (kind, hop - 1),
                        (lax.rem(space + 2 * hop, spatial), chan),
                    ),
                    kind,
                    hop,
                )
            )
        paired.append(send(target.at[space], target.at[space], pair_sems, (kind, 0), partner))
    for q in range(1, groups):
        tell(q)
    for copy in fetched:
        copy.wait()
    for q in range(groups):
        total = 0.0
        for p in range(groups):
            if p > 0:
                arriving[p, q].wait_recv()
                part = landed[p - 1, q]
            else:
                part = feature_v[:, q * extent : (q + 1) * extent]
            source = lax.rem(chan + groups - p, groups)
            columns = pl.ds(pl.multiple_of(source * rows, rows), rows)
            total = total + contract(weight_v[:, columns], part, 1, 0)
        out_ref[q] = total.T
        leaving += spread_block(out_ref, q, q, reach, groups, place, space_sems)
    own = pl.ds(pl.multiple_of(chan * extent, extent), extent)
    state_ref[chan] = feature_v[:, own]
    for p in range(1, groups):
        state_ref[lax.rem(chan + groups - p, groups)] = landed[p - 1, chan]
    for copy, kind, hop in far:
        copy.wait_recv()
        source = lax.rem(space + spatial - 2 * hop, spatial)
        target = shares[kind][1]
        paired.append(send(target.at[source], target.at[source], pair_sems, (kind, hop), partner))
    finish_blocks(out_ref, leaving, reach, groups, place, space_sems)
    for copy in shifts + paired:
        copy.wait()
    for at in range(rows_ref.shape[0]):
        columns_ref[at] = rows_ref[at].T
    for copy in list(arriving.values()) + pieces + [copy for copy, _, _ in far]:
        copy.wait_send()


def mix_states(reach, layer, collected_ref, state_ref, mix_ref, back, sums, heard, place, back_sems, sum_sems):
    space, chan, spatial, groups = place
    order = list(range(1, groups)) + [0]
    copies, returning = [], {}
    for p in order:
        block = lax.rem(chan + p, groups)
        for offset in range(1, reach + 1):
            returning[offset, p] = send(
                collected_ref.at[offset * groups + block],
                back.at[offset - 1, p],
                back_sems,
                (offset - 1, p),
                (lax.rem(space + offset, spatial), chan),
            )
    telling = {}
    for p in order:
        block = lax.rem(chan + p, groups)
        total = collected_ref[block]
        for offset in range(1, reach + 1):
            returning[offset, p].wait_recv()
            total = total + back[offset - 1, p]
        sums[p] = total
        if p > 0:
            telling[p] = send(sums.at[p], heard.at[p - 1], sum_sems, (p - 1,), (space, block))
    copies += list(returning.values()) + list(telling.values())

    def weight(source):
        held = mix_ref[:, source, layer]
        return held.reshape(held.shape[0] * held.shape[1], held.shape[2])

    mixed = contract(weight(chan), sums[0], 1, 1)
    for p in range(1, groups):
        telling[p].wait_recv()
        mixed = mixed + contract(weight(lax.rem(chan + groups - p, groups)), heard[p - 1], 1, 1)
    old = state_ref[...]
    mixed = mixed.reshape(old.shape)
    return old + mixed / (1.0 + jnp.exp(-mixed)), copies


def middle_kernel(
    reach,
    layer,
    collected_ref,
    state_ref,
    mix_ref,
    in_ref,
    out_ref,
    new_ref,
    back,
    sums,
    heard,
    ready,
    *sems,
):
    place = greet(reach)
    space, chan, spatial, groups = place
    new_state, copies = mix_states(
        reach, layer, collected_ref, state_ref, mix_ref, back, sums, heard, place, sems[0:2], sems[2:4]
    )
    new_ref[...] = new_state
    flat = new_state.reshape(new_state.shape[0] * new_state.shape[1], new_state.shape[2])
    handing = {}
    for p in list(range(1, groups)) + [0]:
        target = lax.rem(chan + p, groups)
        held = in_ref[:, target, layer]
        held = held.reshape(held.shape[0] * held.shape[1], held.shape[2])
        mapped = contract(held, flat, 1, 0).T
        if p > 0:
            ready[p - 1] = mapped
            handing[p] = send(ready.at[p - 1], out_ref.at[chan], sems[4:6], (p - 1,), (space, target))
        else:
            out_ref[chan] = mapped
    leaving = spread_block(out_ref, chan, 0, reach, groups, place, sems[6:8])
    for p in range(1, groups):
        handing[p].wait_recv()
        block = lax.rem(chan + groups - p, groups)
        leaving += spread_block(out_ref, block, p, reach, groups, place, sems[6:8])
    finish_blocks(out_ref, leaving, reach, groups, place, sems[6:8])
    for copy in copies + list(handing.values()):
        copy.wait_send()


def last_kernel(reach, layer, collected_ref, state_ref, mix_ref, out_ref, back, sums, heard, ready, *sems):
    place = greet(reach)
    space, chan, spatial, groups = place
    new_state, copies = mix_states(
        reach, layer, collected_ref, state_ref, mix_ref, back, sums, heard, place, sems[0:2], sems[2:4]
    )
    ready[...] = new_state
    extent = ready.shape[2]
    own = pl.ds(pl.multiple_of(chan * extent, extent), extent)
    handing = {}
    for p in range(1, groups):
        target = lax.rem(chan + p, groups)
        handing[p] = send(ready.at[target], out_ref.at[:, own], sems[4:6], (p - 1,), (space, target))
    out_ref[:, own] = ready[chan]
    for p in range(1, groups):
        handing[p].wait_recv()
    for copy in copies + list(handing.values()):
        copy.wait_send()


def remote_call(kernel, outs, scratch, pairs, collective, *operands, elsewhere=0):
    vmem = pl.BlockSpec(memory_space=pltpu.VMEM)
    sems = [pltpu.SemaphoreType.DMA(shape) for shape in pairs for _ in range(2)]
    return pl.pallas_call(
        kernel,
        out_shape=[jax.ShapeDtypeStruct(shape, jnp.float32) for shape in outs],
        in_specs=[vmem] * (len(operands) - elsewhere)
        + [pl.BlockSpec(memory_space=pl.ANY)] * elsewhere,
        out_specs=[vmem] * len(outs),
        scratch_shapes=[pltpu.VMEM(shape, jnp.float32) for shape in scratch] + sems,
        compiler_params=pltpu.CompilerParams(
            collective_id=collective, has_side_effects=True, vmem_limit_bytes=40 * 1024 * 1024
        ),
    )(*operands)


def exchanged_layers(geometry, features, in_weight, mix_weight, reach, pairs_of):
    spatial, groups = lax.axis_size("space"), lax.axis_size("chan")
    blocks, _, block_len = geometry.shape
    channels = features.shape[0]
    slots = (reach + 1) * blocks
    blocked = (slots, block_len, channels)
    held = (groups, channels, block_len)
    square = (block_len, channels)
    hops = spatial // 2
    mix_part = mix_weight.shape[1] // spatial
    in_part = in_weight.shape[1] // spatial
    mapped, state, rows, columns, all_mix, all_in = remote_call(
        functools.partial(gather_kernel, reach),
        [
            blocked,
            held,
            (slots, 8, block_len),
            (slots, block_len, 8),
            (spatial, groups, LAYERS, mix_part, mix_weight.shape[2]),
            (spatial, groups, LAYERS - 1, in_part, in_weight.shape[2]),
        ],
        [(groups - 1, groups, channels, block_len), features.shape, in_weight.shape[1:]],
        [
            (groups - 1, groups),
            (reach, groups),
            (reach,),
            (2, groups - 1),
            (2, hops - 1),
            (2, hops),
            (2,),
        ],
        0,
        geometry,
        features,
        in_weight,
        mix_weight,
        elsewhere=3,
    )
    scratch = [(reach, groups, *square), (groups, *square), (groups - 1, *square)]
    for layer in range(LAYERS - 1):
        collected = pairs_of(columns, rows, mapped, layer)
        mapped, state = remote_call(
            functools.partial(middle_kernel, reach, layer),
            [blocked, held],
            scratch + [(groups - 1, *square)],
            [(reach, groups), (groups - 1,), (groups - 1,), (reach, groups)],
            1,
            collected,
            state,
            all_mix,
            all_in,
        )
    collected = pairs_of(columns, rows, mapped, LAYERS - 1)
    (updated,) = remote_call(
        functools.partial(last_kernel, reach, LAYERS - 1),
        [features.shape],
        scratch + [held],
        [(reach, groups), (groups - 1,), (groups - 1,)],
        2,
        collected,
        state,
        all_mix,
    )
    return updated


def shards(positions, features, block_counts, pair_table, in_weight, filter_weight, mix_weight):
    spatial = lax.axis_size("space")
    reach_dev = spatial // 4
    own_index = lax.axis_index("space")
    blocks = block_counts.shape[0]
    atoms_dev = positions.shape[1]
    block_len = atoms_dev // blocks
    local_chan = features.shape[0]
    slot_total = (reach_dev + 1) * blocks
    valid = (
        (lax.broadcasted_iota(jnp.int32, (blocks, block_len), 1) < block_counts[:, None])
        .astype(jnp.float32)
        .reshape(1, atoms_dev)
    )
    geometry = jnp.concatenate([positions, valid, jnp.zeros((4, atoms_dev), jnp.float32)], axis=0)
    geometry = geometry.reshape(8, blocks, block_len).transpose(1, 0, 2)
    base = jnp.stack([own_index, jnp.int32(spatial)]).astype(jnp.int32)
    groups = lax.axis_size("chan")

    def pairs_of(columns, rows, mapped_blocks, layer):
        return pair_messages(
            base, pair_table, columns, rows, mapped_blocks, filter_weight[layer], blocks
        )

    whole_tiles = (
        local_chan % 128 == 0
        and block_len % 128 == 0
        and blocks == groups
        and spatial > 2 * reach_dev
        and spatial % 2 == 0
        and local_chan % (8 * spatial) == 0
    )
    if whole_tiles:
        return exchanged_layers(geometry, features, in_weight, mix_weight, reach_dev, pairs_of)
    fetched = [geometry]
    for offset in range(1, reach_dev + 1):
        fetched.append(shifted(geometry, "space", -offset))
    rows = jnp.concatenate(fetched, axis=0)
    columns = rows.transpose(0, 2, 1)
    state = features
    for layer in range(LAYERS):
        full_state = lax.all_gather(state, "chan", axis=0, tiled=True)
        mapped = lax.dot_general(
            full_state,
            in_weight[layer],
            (((0,), (1,)), ((), ())),
            precision=lax.Precision.HIGHEST,
            preferred_element_type=jnp.float32,
        )
        neighbours = [mapped]
        for offset in range(1, reach_dev + 1):
            neighbours.append(shifted(mapped, "space", -offset))
        mapped_blocks = jnp.concatenate(neighbours, axis=0).reshape(slot_total, block_len, local_chan)
        collected = pairs_of(columns, rows, mapped_blocks, layer).reshape(reach_dev + 1, atoms_dev, local_chan)
        received = collected[0]
        for offset in range(1, reach_dev + 1):
            received = received + shifted(collected[offset], "space", offset)
        mixed = lax.dot_general(
            mix_weight[layer],
            received,
            (((1,), (1,)), ((), ())),
            precision=lax.Precision.HIGHEST,
            preferred_element_type=jnp.float32,
        )
        own_mixed = lax.psum_scatter(mixed, "chan", scatter_dimension=0, tiled=True)
        state = state + jax.nn.silu(own_mixed)
    return state


def solution(mesh):
    placed = (
        P(None, "space"),
        P("chan", "space"),
        P("space"),
        P(None, "space"),
        P(None, "chan", None),
        P(None, None, "chan"),
        P(None, None, "chan"),
    )
    return jax.shard_map(
        shards, mesh=mesh, in_specs=placed, out_specs=P("chan", "space"), check_vma=False
    )
```

```python
import functools
import math

import jax
import jax.numpy as jnp
from jax import lax
from jax.experimental import pallas as pl
from jax.experimental.pallas import tpu as pltpu
from jax.sharding import PartitionSpec as P

K = 8
LAYERS = 2


cutoff_radius = 6.0
gamma_width = 1.5
spacing = cutoff_radius / (K - 1)


def shifted(block, axis, distance):
    devices = range(lax.axis_size(axis))
    route = [((i - distance) % len(devices), i) for i in devices]
    return lax.ppermute(block, axis, route)


def half_cosine(y):
    terms = [(-1) ** n * (math.pi / 2) ** (2 * n) / math.factorial(2 * n) for n in range(8)]
    total = jnp.full_like(y, terms[-1])
    for term in terms[-2::-1]:
        total = total * y + term
    return total


def split_halves(value):
    high = value.astype(jnp.bfloat16)
    low = (value - high.astype(jnp.float32)).astype(jnp.bfloat16)
    return high, low


def write_basis(columns, rows, weight, same, out):
    squared = 0.0
    for axis in range(3):
        offset = columns[:, axis : axis + 1] - rows[axis : axis + 1, :]
        squared = squared + offset * offset
    extent = squared.shape[0]
    limit = cutoff_radius * cutoff_radius
    near = jnp.minimum(squared, limit)
    distance = jnp.sqrt(near)
    root = half_cosine(near * (1.0 / limit))
    allowed = (columns[:, 3:4] * weight) * rows[3:4, :]
    diagonal = lax.broadcasted_iota(jnp.int32, (extent, extent), 0) == lax.broadcasted_iota(
        jnp.int32, (extent, extent), 1
    )
    dropped = (squared >= limit) | (diagonal & same)
    envelope = jnp.where(dropped, 0.0, root * root * allowed)
    middle = K // 2 - 1
    spread = distance - middle * spacing
    centre = jnp.exp(-gamma_width * spread * spread) * envelope
    slope = 2.0 * gamma_width * spacing
    up = jnp.exp(slope * distance)
    down = jnp.exp(-slope * distance)

    def put(k, value):
        high, low = split_halves(value)
        out[k * extent : (k + 1) * extent, :extent] = high
        out[k * extent : (k + 1) * extent, extent:] = low

    put(middle, centre)
    unit = gamma_width * spacing * spacing
    value = centre
    for k in range(middle + 1, K):
        value = value * (up * math.exp(-unit * (2 * k - 1)))
        put(k, value)
    value = centre
    for k in range(middle - 1, -1, -1):
        value = value * (down * math.exp(unit * (2 * k + 1)))
        put(k, value)


def pair_kernel(
    blocks,
    base_ref,
    table_ref,
    columns_ref,
    rows_ref,
    mapped_ref,
    filter_ref,
    turned_ref,
    out_ref,
    count_s,
    to_s,
    from_s,
    weight_s,
    operand_v,
    scaled_v,
    other_v,
    basis_a,
    basis_b,
):
    slots, extent, channels = mapped_ref.shape
    spatial = base_ref[1]
    own = base_ref[0]

    def clear(i, carry):
        count_s[i] = 0
        return carry

    lax.fori_loop(0, blocks * slots, clear, 0)

    def tally(p, carry):
        first = table_ref[0, p] - own * blocks
        second = table_ref[1, p]
        holder = second // blocks
        ahead = holder - own
        ahead = jnp.where(ahead < 0, ahead + spatial, ahead)
        second = ahead * blocks + (second - holder * blocks)
        swap = second < first
        at = jnp.where(swap, second, first) * slots + jnp.where(swap, first, second)
        count_s[at] = count_s[at] + table_ref[2, p]
        return carry

    lax.fori_loop(0, table_ref.shape[1], tally, 0)

    def list_row(first, n):
        def list_one(second, n):
            many = count_s[first * slots + second]
            to_s[n] = first
            from_s[n] = second
            weight_s[n] = many.astype(jnp.float32)
            return n + (many > 0).astype(jnp.int32)

        return lax.fori_loop(first, slots, list_one, n)

    total = lax.fori_loop(0, blocks, list_row, 0)
    for extra in range(3):
        to_s[total + extra] = 0
        from_s[total + extra] = 0
        weight_s[total + extra] = 0.0

    for slot in range(slots):
        high, low = split_halves(mapped_ref[slot])
        for part in range(2):
            operand_v[slot, part * extent : (part + 1) * extent, :channels] = high
            operand_v[slot, part * extent : (part + 1) * extent, channels:] = low
    for slot in range(blocks):
        turned = mapped_ref[slot].T
        for k in range(K):
            high, low = split_halves(turned * turned_ref[:, k : k + 1])
            scaled_v[slot, :channels, k * extent : (k + 1) * extent] = high
            scaled_v[slot, channels:, k * extent : (k + 1) * extent] = low
    out_ref[...] = jnp.zeros_like(out_ref)
    other_v[...] = jnp.zeros_like(other_v)

    def build(task, basis):
        to, source = to_s[task], from_s[task]
        write_basis(columns_ref[to], rows_ref[source], weight_s[task], to == source, basis)

    def spend(task, basis):
        to, source = to_s[task], from_s[task]
        product = jnp.dot(basis[...], operand_v[source], preferred_element_type=jnp.float32)
        summed = 0.0
        for k in range(K):
            part = product[k * extent : (k + 1) * extent]
            summed = summed + filter_ref[k : k + 1, :] * (part[:, :channels] + part[:, channels:])
        out_ref[to] = out_ref[to] + summed
        both = jnp.dot(scaled_v[to], basis[...], preferred_element_type=jnp.float32)
        back = both[:channels] + both[channels:]
        back = back[:, :extent] + back[:, extent:]
        other_v[source] = other_v[source] + back * jnp.where(to == source, 0.0, 1.0)

    build(0, basis_a)

    def step(turn, carry):
        task = 2 * turn
        build(task + 1, basis_b)
        spend(task, basis_a)
        build(task + 2, basis_a)
        spend(task + 1, basis_b)
        return carry

    lax.fori_loop(0, (total + 1) // 2, step, 0)
    for slot in range(slots):
        out_ref[slot] = out_ref[slot] + other_v[slot].T


def pair_messages(base, table, columns, rows, mapped, filters, blocks, interpret=False):
    slots, extent, channels = mapped.shape
    tasks = blocks * slots + 8
    smem = pl.BlockSpec(memory_space=pltpu.SMEM)
    vmem = pl.BlockSpec(memory_space=pltpu.VMEM)
    return pl.pallas_call(
        functools.partial(pair_kernel, blocks),
        out_shape=jax.ShapeDtypeStruct(mapped.shape, jnp.float32),
        in_specs=[smem, smem, vmem, vmem, vmem, vmem, vmem],
        out_specs=vmem,
        scratch_shapes=[
            pltpu.SMEM((blocks * slots,), jnp.int32),
            pltpu.SMEM((tasks,), jnp.int32),
            pltpu.SMEM((tasks,), jnp.int32),
            pltpu.SMEM((tasks,), jnp.float32),
            pltpu.VMEM((slots, 2 * extent, 2 * channels), jnp.bfloat16),
            pltpu.VMEM((blocks, 2 * channels, K * extent), jnp.bfloat16),
            pltpu.VMEM((slots, channels, extent), jnp.float32),
            pltpu.VMEM((K * extent, 2 * extent), jnp.bfloat16),
            pltpu.VMEM((K * extent, 2 * extent), jnp.bfloat16),
        ],
        compiler_params=pltpu.CompilerParams(vmem_limit_bytes=48 * 1024 * 1024),
        interpret=interpret,
    )(base, table, columns, rows, mapped, filters, filters.T)


MESH = pl.DeviceIdType.MESH


def contract(left, right, left_dim, right_dim):
    left, right = split_halves(left), split_halves(right)
    total = 0.0
    for one, other in ((0, 0), (0, 1), (1, 0)):
        total = total + lax.dot_general(
            left[one],
            right[other],
            (((left_dim,), (right_dim,)), ((), ())),
            preferred_element_type=jnp.float32,
        )
    return total


def greet(reach, stride=None):
    space, chan = lax.axis_index("space"), lax.axis_index("chan")
    spatial, groups = lax.axis_size("space"), lax.axis_size("chan")
    barrier = pltpu.get_barrier_semaphore()
    partners = [(space, lax.rem(chan + p, groups)) for p in range(1, groups)]
    offsets = set(range(1, reach + 1)) | {spatial - offset for offset in range(1, reach + 1)}
    if stride is not None:
        offsets |= set(range(stride, spatial, stride))
    for offset in sorted(offsets):
        partners.append((lax.rem(space + offset, spatial), chan))
    for partner in partners:
        pl.semaphore_signal(barrier, inc=1, device_id=partner, device_id_type=MESH)
    pl.semaphore_wait(barrier, len(partners))
    return space, chan, spatial, groups


def send(source, target, sems, at, device):
    copy = pltpu.make_async_remote_copy(
        src_ref=source,
        dst_ref=target,
        send_sem=sems[0].at[at],
        recv_sem=sems[1].at[at],
        device_id=device,
        device_id_type=MESH,
    )
    copy.start()
    return copy


def spread_block(out_ref, block, p, reach, blocks, place, sems):
    space, chan, spatial, groups = place
    copies = {}
    for offset in range(1, reach + 1):
        copies[offset] = pltpu.make_async_remote_copy(
            src_ref=out_ref.at[block],
            dst_ref=out_ref.at[offset * blocks + block],
            send_sem=sems[0].at[offset - 1, p],
            recv_sem=sems[1].at[offset - 1, p],
            device_id=(lax.rem(space + spatial - offset, spatial), chan),
            device_id_type=MESH,
        )
        if offset == 1 and reach > 1:
            pl.when(lax.rem(space, 2) == 1)(copies[offset].start)
        else:
            copies[offset].start()
    return [(block, p, copies)]


def finish_blocks(out_ref, leaving, reach, blocks, place, sems):
    space, chan, spatial, groups = place
    for block, p, copies in leaving:
        if reach > 1:
            copies[2].wait_recv()
            onward = pltpu.make_async_remote_copy(
                src_ref=out_ref.at[2 * blocks + block],
                dst_ref=out_ref.at[blocks + block],
                send_sem=sems[0].at[0, p],
                recv_sem=sems[1].at[0, p],
                device_id=(lax.rem(space + 1, spatial), chan),
                device_id_type=MESH,
            )
            pl.when(lax.rem(space, 2) == 0)(onward.start)
    for block, p, copies in leaving:
        for offset, copy in copies.items():
            if offset != 2:
                copy.wait_recv()
            copy.wait_send()


def gather_kernel(
    reach,
    geometry_ref,
    feature_ref,
    weight_ref,
    mix_ref,
    out_ref,
    state_ref,
    rows_ref,
    columns_ref,
    all_mix_ref,
    all_in_ref,
    landed,
    feature_v,
    weight_v,
    *sems,
):
    place = greet(reach, 2)
    space, chan, spatial, groups = place
    chan_sems, space_sems, near_sems, piece_sems, far_sems, pair_sems, own_sems = (
        sems[2 * i : 2 * i + 2] for i in range(7)
    )
    fetched = [
        pltpu.make_async_copy(feature_ref, feature_v, own_sems[0].at[0]),
        pltpu.make_async_copy(weight_ref.at[0], weight_v, own_sems[0].at[1]),
    ]
    for copy in fetched:
        copy.start()
    rows, _ = feature_ref.shape
    extent = out_ref.shape[1]
    blocks = geometry_ref.shape[0]

    shares = []
    for source, target in ((mix_ref, all_mix_ref), (weight_ref, all_in_ref)):
        part = target.shape[-2]
        mine = pl.ds(pl.multiple_of(space * part, part), part)
        if target is all_in_ref:
            held = source.at[pl.ds(1, LAYERS - 1), mine]
        else:
            held = source.at[:, mine]
        shares.append((held, target))
    pieces, leaving, shifts = [], [], []
    for p in range(1, groups):
        for kind, (held, target) in enumerate(shares):
            pieces.append(
                send(
                    held,
                    target.at[space, chan],
                    piece_sems,
                    (kind, p - 1),
                    (space, lax.rem(chan + p, groups)),
                )
            )
    rows_ref[:blocks] = geometry_ref[...]
    for offset in range(1, reach + 1):
        shifts.append(
            send(
                geometry_ref,
                rows_ref.at[pl.ds(offset * blocks, blocks)],
                near_sems,
                (offset - 1,),
                (lax.rem(space + spatial - offset, spatial), chan),
            )
        )
    arriving = {}

    def tell(q):
        for p in range(1, groups):
            arriving[p, q] = send(
                feature_ref.at[:, q * extent : (q + 1) * extent],
                landed.at[p - 1, q],
                chan_sems,
                (p - 1, q),
                (space, lax.rem(chan + p, groups)),
            )

    tell(0)
    kept = []
    for kind, (held, target) in enumerate(shares):
        kept.append(pltpu.make_async_copy(held, target.at[space, chan], own_sems[1].at[kind]))
        kept[-1].start()
    for copy in kept:
        copy.wait()
    for copy in pieces:
        copy.wait_recv()
    far, paired = [], []
    partner = (space + 1 - 2 * lax.rem(space, 2), chan)
    for kind, (_, target) in enumerate(shares):
        for hop in range(1, spatial // 2):
            far.append(
                (
                    send(
                        target.at[space],
                        target.at[space],
                        far_sems,
                        (kind, hop - 1),
                        (lax.rem(space + 2 * hop, spatial), chan),
                    ),
                    kind,
                    hop,
                )
            )
        paired.append(send(target.at[space], target.at[space], pair_sems, (kind, 0), partner))
    for q in range(1, groups):
        tell(q)
    for copy in fetched:
        copy.wait()
    for q in range(groups):
        total = 0.0
        for p in range(groups):
            if p > 0:
                arriving[p, q].wait_recv()
                part = landed[p - 1, q]
            else:
                part = feature_v[:, q * extent : (q + 1) * extent]
            source = lax.rem(chan + groups - p, groups)
            columns = pl.ds(pl.multiple_of(source * rows, rows), rows)
            total = total + contract(weight_v[:, columns], part, 1, 0)
        out_ref[q] = total.T
        leaving += spread_block(out_ref, q, q, reach, groups, place, space_sems)
    own = pl.ds(pl.multiple_of(chan * extent, extent), extent)
    state_ref[chan] = feature_v[:, own]
    for p in range(1, groups):
        state_ref[lax.rem(chan + groups - p, groups)] = landed[p - 1, chan]
    for copy, kind, hop in far:
        copy.wait_recv()
        source = lax.rem(space + spatial - 2 * hop, spatial)
        target = shares[kind][1]
        paired.append(send(target.at[source], target.at[source], pair_sems, (kind, hop), partner))
    finish_blocks(out_ref, leaving, reach, groups, place, space_sems)
    for copy in shifts + paired:
        copy.wait()
    for at in range(rows_ref.shape[0]):
        columns_ref[at] = rows_ref[at].T
    for copy in list(arriving.values()) + pieces + [copy for copy, _, _ in far]:
        copy.wait_send()


def mix_states(reach, layer, collected_ref, state_ref, mix_ref, back, sums, heard, place, back_sems, sum_sems):
    space, chan, spatial, groups = place
    order = list(range(1, groups)) + [0]
    copies, returning = [], {}
    for p in order:
        block = lax.rem(chan + p, groups)
        for offset in range(1, reach + 1):
            returning[offset, p] = send(
                collected_ref.at[offset * groups + block],
                back.at[offset - 1, p],
                back_sems,
                (offset - 1, p),
                (lax.rem(space + offset, spatial), chan),
            )
    telling = {}
    for p in order:
        block = lax.rem(chan + p, groups)
        total = collected_ref[block]
        for offset in range(1, reach + 1):
            returning[offset, p].wait_recv()
            total = total + back[offset - 1, p]
        sums[p] = total
        if p > 0:
            telling[p] = send(sums.at[p], heard.at[p - 1], sum_sems, (p - 1,), (space, block))
    copies += list(returning.values()) + list(telling.values())

    def weight(source):
        held = mix_ref[:, source, layer]
        return held.reshape(held.shape[0] * held.shape[1], held.shape[2])

    mixed = contract(weight(chan), sums[0], 1, 1)
    for p in range(1, groups):
        telling[p].wait_recv()
        mixed = mixed + contract(weight(lax.rem(chan + groups - p, groups)), heard[p - 1], 1, 1)
    old = state_ref[...]
    mixed = mixed.reshape(old.shape)
    return old + mixed / (1.0 + jnp.exp(-mixed)), copies


def middle_kernel(
    reach,
    layer,
    collected_ref,
    state_ref,
    mix_ref,
    in_ref,
    out_ref,
    new_ref,
    back,
    sums,
    heard,
    ready,
    *sems,
):
    place = greet(reach)
    space, chan, spatial, groups = place
    new_state, copies = mix_states(
        reach, layer, collected_ref, state_ref, mix_ref, back, sums, heard, place, sems[0:2], sems[2:4]
    )
    new_ref[...] = new_state
    flat = new_state.reshape(new_state.shape[0] * new_state.shape[1], new_state.shape[2])
    handing = {}
    for p in list(range(1, groups)) + [0]:
        target = lax.rem(chan + p, groups)
        held = in_ref[:, target, layer]
        held = held.reshape(held.shape[0] * held.shape[1], held.shape[2])
        mapped = contract(held, flat, 1, 0).T
        if p > 0:
            ready[p - 1] = mapped
            handing[p] = send(ready.at[p - 1], out_ref.at[chan], sems[4:6], (p - 1,), (space, target))
        else:
            out_ref[chan] = mapped
    leaving = spread_block(out_ref, chan, 0, reach, groups, place, sems[6:8])
    for p in range(1, groups):
        handing[p].wait_recv()
        block = lax.rem(chan + groups - p, groups)
        leaving += spread_block(out_ref, block, p, reach, groups, place, sems[6:8])
    finish_blocks(out_ref, leaving, reach, groups, place, sems[6:8])
    for copy in copies + list(handing.values()):
        copy.wait_send()


def last_kernel(reach, layer, collected_ref, state_ref, mix_ref, out_ref, back, sums, heard, ready, *sems):
    place = greet(reach)
    space, chan, spatial, groups = place
    new_state, copies = mix_states(
        reach, layer, collected_ref, state_ref, mix_ref, back, sums, heard, place, sems[0:2], sems[2:4]
    )
    ready[...] = new_state
    extent = ready.shape[2]
    own = pl.ds(pl.multiple_of(chan * extent, extent), extent)
    handing = {}
    for p in range(1, groups):
        target = lax.rem(chan + p, groups)
        handing[p] = send(ready.at[target], out_ref.at[:, own], sems[4:6], (p - 1,), (space, target))
    out_ref[:, own] = ready[chan]
    for p in range(1, groups):
        handing[p].wait_recv()
    for copy in copies + list(handing.values()):
        copy.wait_send()


def remote_call(kernel, outs, scratch, pairs, collective, *operands, elsewhere=0, grant=40):
    vmem = pl.BlockSpec(memory_space=pltpu.VMEM)
    sems = [pltpu.SemaphoreType.DMA(shape) for shape in pairs for _ in range(2)]
    return pl.pallas_call(
        kernel,
        out_shape=[jax.ShapeDtypeStruct(shape, jnp.float32) for shape in outs],
        in_specs=[vmem] * (len(operands) - elsewhere)
        + [pl.BlockSpec(memory_space=pl.ANY)] * elsewhere,
        out_specs=[vmem] * len(outs),
        scratch_shapes=[pltpu.VMEM(shape, jnp.float32) for shape in scratch] + sems,
        compiler_params=pltpu.CompilerParams(
            collective_id=collective, has_side_effects=True, vmem_limit_bytes=grant * 1024 * 1024
        ),
    )(*operands)


def exchanged_layers(geometry, features, in_weight, mix_weight, reach, pairs_of):
    spatial, groups = lax.axis_size("space"), lax.axis_size("chan")
    blocks, _, block_len = geometry.shape
    channels = features.shape[0]
    slots = (reach + 1) * blocks
    blocked = (slots, block_len, channels)
    held = (groups, channels, block_len)
    square = (block_len, channels)
    hops = spatial // 2
    mix_part = mix_weight.shape[1] // spatial
    in_part = in_weight.shape[1] // spatial
    mapped, state, rows, columns, all_mix, all_in = remote_call(
        functools.partial(gather_kernel, reach),
        [
            blocked,
            held,
            (slots, 8, block_len),
            (slots, block_len, 8),
            (spatial, groups, LAYERS, mix_part, mix_weight.shape[2]),
            (spatial, groups, LAYERS - 1, in_part, in_weight.shape[2]),
        ],
        [(groups - 1, groups, channels, block_len), features.shape, in_weight.shape[1:]],
        [
            (groups - 1, groups),
            (reach, groups),
            (reach,),
            (2, groups - 1),
            (2, hops - 1),
            (2, hops),
            (2,),
        ],
        0,
        geometry,
        features,
        in_weight,
        mix_weight,
        elsewhere=3,
        grant=60,
    )
    scratch = [(reach, groups, *square), (groups, *square), (groups - 1, *square)]
    for layer in range(LAYERS - 1):
        collected = pairs_of(columns, rows, mapped, layer)
        mapped, state = remote_call(
            functools.partial(middle_kernel, reach, layer),
            [blocked, held],
            scratch + [(groups - 1, *square)],
            [(reach, groups), (groups - 1,), (groups - 1,), (reach, groups)],
            1,
            collected,
            state,
            all_mix,
            all_in,
        )
    collected = pairs_of(columns, rows, mapped, LAYERS - 1)
    (updated,) = remote_call(
        functools.partial(last_kernel, reach, LAYERS - 1),
        [features.shape],
        scratch + [held],
        [(reach, groups), (groups - 1,), (groups - 1,)],
        2,
        collected,
        state,
        all_mix,
    )
    return updated


def shards(positions, features, block_counts, pair_table, in_weight, filter_weight, mix_weight):
    spatial = lax.axis_size("space")
    reach_dev = spatial // 4
    own_index = lax.axis_index("space")
    blocks = block_counts.shape[0]
    atoms_dev = positions.shape[1]
    block_len = atoms_dev // blocks
    local_chan = features.shape[0]
    slot_total = (reach_dev + 1) * blocks
    valid = (
        (lax.broadcasted_iota(jnp.int32, (blocks, block_len), 1) < block_counts[:, None])
        .astype(jnp.float32)
        .reshape(1, atoms_dev)
    )
    geometry = jnp.concatenate([positions, valid, jnp.zeros((4, atoms_dev), jnp.float32)], axis=0)
    geometry = geometry.reshape(8, blocks, block_len).transpose(1, 0, 2)
    base = jnp.stack([own_index, jnp.int32(spatial)]).astype(jnp.int32)
    groups = lax.axis_size("chan")

    def pairs_of(columns, rows, mapped_blocks, layer):
        return pair_messages(
            base, pair_table, columns, rows, mapped_blocks, filter_weight[layer], blocks
        )

    whole_tiles = (
        local_chan % 128 == 0
        and block_len % 128 == 0
        and blocks == groups
        and spatial > 2 * reach_dev
        and spatial % 2 == 0
        and local_chan % (8 * spatial) == 0
    )
    if whole_tiles:
        return exchanged_layers(geometry, features, in_weight, mix_weight, reach_dev, pairs_of)
    fetched = [geometry]
    for offset in range(1, reach_dev + 1):
        fetched.append(shifted(geometry, "space", -offset))
    rows = jnp.concatenate(fetched, axis=0)
    columns = rows.transpose(0, 2, 1)
    state = features
    for layer in range(LAYERS):
        full_state = lax.all_gather(state, "chan", axis=0, tiled=True)
        mapped = lax.dot_general(
            full_state,
            in_weight[layer],
            (((0,), (1,)), ((), ())),
            precision=lax.Precision.HIGHEST,
            preferred_element_type=jnp.float32,
        )
        neighbours = [mapped]
        for offset in range(1, reach_dev + 1):
            neighbours.append(shifted(mapped, "space", -offset))
        mapped_blocks = jnp.concatenate(neighbours, axis=0).reshape(slot_total, block_len, local_chan)
        collected = pairs_of(columns, rows, mapped_blocks, layer).reshape(reach_dev + 1, atoms_dev, local_chan)
        received = collected[0]
        for offset in range(1, reach_dev + 1):
            received = received + shifted(collected[offset], "space", offset)
        mixed = lax.dot_general(
            mix_weight[layer],
            received,
            (((1,), (1,)), ((), ())),
            precision=lax.Precision.HIGHEST,
            preferred_element_type=jnp.float32,
        )
        own_mixed = lax.psum_scatter(mixed, "chan", scatter_dimension=0, tiled=True)
        state = state + jax.nn.silu(own_mixed)
    return state


def solution(mesh):
    placed = (
        P(None, "space"),
        P("chan", "space"),
        P("space"),
        P(None, "space"),
        P(None, "chan", None),
        P(None, None, "chan"),
        P(None, None, "chan"),
    )
    return jax.shard_map(
        shards, mesh=mesh, in_specs=placed, out_specs=P("chan", "space"), check_vma=False
    )
```
